32 devices in a mesh: section: 2 (over core), dp: 8 (over z, y), tensor: 2 (over x).
Axes of the slice: x: 2, y: 2, z: 4, core: 2. Of those that a mesh axis runs over, the one named last changes fastest.
Arguments:
- layer_inputs: bfloat16 [2, 16, 512, 1024], P('section', 'dp', None, 'tensor'), may hold values from -6 to 6
- output_cotangents: bfloat16 [2, 16, 512, 1024], P('section', 'dp', None, 'tensor'), may hold values from -6 to 6
- segment_ids: int32 [2, 16, 512], P(None, 'dp'), may hold values from 0 to 3, never falling along the last dimension, each value on 1 to 256 neighbouring positions
- attention_in: bfloat16 [2, 1024, 3, 1024], P('section', None, None, 'tensor'), may hold values from -0.1875 to 0.1875
- attention_out: bfloat16 [2, 1024, 1024], P('section', 'tensor'), may hold values from -1.5 to 1.5
- cross_weights: bfloat16 [2, 1024, 2, 1024], P('section', None, None, 'tensor'), may hold values from -0.875 to 0.875
- expand_weights: bfloat16 [2, 1024, 4096], P('section', None, 'tensor'), may hold values from -0.1875 to 0.1875
- contract_weights: bfloat16 [2, 4096, 1024], P('section', 'tensor'), may hold values from -0.125 to 0.125
- norm_gains: float32 [2, 3, 1024], P('section', None, 'tensor'), may hold values from 0.25 to 1.75
- bias_tables: float32 [2, 32, 16], P('section', None, 'tensor'), may hold values from -1.5 to 1.5
Outputs:
- layer_outputs: float32 [2, 16, 512, 1024], P('section', 'dp', None, 'tensor')
- input_gradient: float32 [2, 16, 512, 1024], P('section', 'dp', None, 'tensor')
- attention_in_gradient: float32 [2, 1024, 3, 1024], P('section', None, None, 'tensor')
- attention_out_gradient: float32 [2, 1024, 1024], P('section', 'tensor')
- cross_gradient: float32 [2, 1024, 2, 1024], P('section', None, None, 'tensor')
- expand_gradient: float32 [2, 1024, 4096], P('section', None, 'tensor')
- contract_gradient: float32 [2, 4096, 1024], P('section', 'tensor')
- gains_gradient: float32 [2, 3, 1024], P('section', None, 'tensor')
- bias_gradient: float32 [2, 32, 16], P('section', None, 'tensor')
The draws below stay inside these ranges and needn't reach their ends.
Inputs may be any that keep to these rules, and one draw needn't show every extreme that they name: `segment_ids`: in each row the numbers never fall and every number of 0 to 3 occurs.
All inputs are finite; a program needn't handle non-finite values.
Results may differ from the reference program's by a relative error of at most 0.025.
Values may be sent and summed in bfloat16 or wider, within the bound.
No kernel may reach another device: no remote copies, remote signals or barrier semaphores. Data moves between devices by JAX's collectives and lax.ppermute only.
A program may use at most 256 MiB of HBM per device.

```python
import math
import jax
import jax.numpy as jnp
import numpy as np
from jax import lax

D = 1024
H = 16
HEAD = 64
FF = 4096
BUCKETS = 32
MAXDIST = 128
LEN = 512
SEGS = 4
ROWS = 16
N_DP = 8


def draw_cross_weights(key, part):
    key = jax.random.fold_in(key, 5)
    base = jnp.clip(jax.random.normal(key, (2, D, 2, H * HEAD), jnp.float32), -3.5, 3.5) * D ** (-0.5)
    factor = jnp.ones((2, 1, 2, 1), jnp.float32).at[1, 0, 1, 0].set(8.0)
    return (base * factor).astype(jnp.bfloat16)


def block_scale(key, extent, pieces, least, top_value):
    factor_of, own = 1.0, jax.random.fold_in(key, 6)
    for position, blocks in pieces:
        steps = jnp.exp(jax.random.uniform(jax.random.fold_in(own, position), (blocks,), jnp.float32, least / len(pieces), top_value / len(pieces)))
        factor_of = factor_of * jnp.repeat(steps, extent[position] // blocks).reshape([-1 if axis == position else 1 for axis in range(len(extent))])
    return factor_of


def profile(count, total, limit, lean):
    portions = [(1 << 20) // math.isqrt(standing ** lean) + 1 for standing in range(2, count + 1)]
    rest, counts = total - limit - (count - 1), [1] * (count - 1)
    while rest > 0:
        movable = [i for i in range(count - 1) if counts[i] < limit]
        pool, left = sum([portions[i] for i in movable]), rest
        for i in movable:
            addition = min(limit - counts[i], max(1, left * portions[i] // pool), rest)
            counts[i] = counts[i] + addition
            rest = rest - addition
    return np.array([limit] + counts)


def uneven(rng, count, total, limit, lean):
    if count == 2:
        one = jax.random.randint(rng, (), max(1, total - limit), min(limit, total - 1) + 1)
        return jnp.stack([one, total - one])
    lengths = jnp.asarray(profile(count, total, limit, lean), jnp.int32)
    twos = (count - 1) // 2
    source_of, sink = lengths[1:1 + 2 * twos:2], lengths[2:2 + 2 * twos:2]
    margin = jnp.minimum(source_of - 1, limit - sink)
    passed = jax.random.randint(jax.random.fold_in(rng, 1), (twos,), 0, 1 << 20) % (margin + 1)
    lengths = lengths.at[1:1 + 2 * twos:2].set(source_of - passed).at[2:2 + 2 * twos:2].set(sink + passed)
    return lengths[jax.random.permutation(jax.random.fold_in(rng, 2), count)]


def centred(rng, extent, width, bound, pieces=(), held_as=jnp.bfloat16):
    level = block_scale(rng, extent, pieces, -0.22, 0.18) if pieces else 1.0
    values = jax.random.normal(rng, extent, jnp.float32) * width * level
    return jnp.minimum(jnp.maximum(values, -bound), bound).astype(held_as)


def setup_inputs(seed: int = 0) -> dict:
    splits = jax.random.split(jax.random.key(seed), 11)
    return {
        "layer_inputs": centred(splits[0], (2, ROWS, LEN, D), 1.0, 6.0, ((0, 2), (1, 8), (3, 2))),
        "output_cotangents": centred(splits[1], (2, ROWS, LEN, D), 1.0, 6.0, ((0, 2), (1, 8), (3, 2))),
        "segment_ids": jax.vmap(lambda own: jnp.searchsorted(jnp.cumsum(uneven(own, SEGS, LEN, LEN // 2, 2)), jnp.arange(LEN), side="right"))(jax.random.split(splits[2], 2 * ROWS)).reshape((2, ROWS, LEN)).astype(jnp.int32),
        "attention_in": centred(splits[3], (2, D, 3, H * HEAD), D ** -0.5, 0.1875, ((0, 2), (3, 2))),
        "attention_out": centred(splits[4], (2, H * HEAD, D), (H * HEAD // 64) ** -0.5, 1.5, ((0, 2), (1, 2))),
        "cross_weights": draw_cross_weights(jax.random.fold_in(splits[10], 71), 0),
        "expand_weights": centred(splits[6], (2, D, FF), D ** -0.5, 0.1875, ((0, 2), (2, 2))),
        "contract_weights": centred(splits[7], (2, FF, D), (FF // 2) ** -0.5, 0.125, ((0, 2), (1, 2))),
        "norm_gains": jnp.clip(1.0 + 0.15 * jax.random.normal(splits[8], (2, 3, D), jnp.float32), 0.25, 1.75),
        "bias_tables": jnp.clip(jax.random.uniform(splits[9], (2, BUCKETS, H), jnp.float32, -1.5, 1.5) * block_scale(splits[9], (2, BUCKETS, H), ((0, 2), (2, 2)), -0.4, 0.0), -1.5, 1.5),
    }


epsilon = 1e-06
masked_score = -1e+30
highest = lax.Precision.HIGHEST

@jax.custom_vjp
def low(v):
    return lax.optimization_barrier(v.astype(jnp.bfloat16)).astype(jnp.float32)

@jax.custom_vjp
def low_back(v):
    return v

def low_keep(v):
    return (low(v), None)

def low_pass(kept, grad):
    return (grad,)

def back_keep(v):
    return (v, None)

def back_low(kept, grad):
    return (low(grad),)
low.defvjp(low_keep, low_pass)
low_back.defvjp(back_keep, back_low)

def both_ways(value):
    return low(low_back(value))

def bucket_matrix(length, causal):
    count = BUCKETS if causal else BUCKETS // 2
    exact = count // 2
    distance = np.arange(length)
    spread = exact + (np.log(np.maximum(distance, 1) / exact) / np.log(MAXDIST / exact) * (count - exact)).astype(np.int64)
    levels = np.where(distance < exact, distance, np.minimum(spread, count - 1))
    breaks = [int(np.argmax(levels >= level)) for level in range(1, count) if bool((levels >= level).any())]
    offset = jnp.arange(length, dtype=jnp.int32)[None, :] - jnp.arange(length, dtype=jnp.int32)[:, None]
    if causal:
        reach = jnp.maximum(-offset, 0)
        bucket = jnp.zeros((length, length), jnp.int32)
    else:
        reach = jnp.abs(offset)
        bucket = jnp.where(offset > 0, count, 0).astype(jnp.int32)
    for edge in breaks:
        bucket = bucket + (reach >= edge).astype(jnp.int32)
    return bucket

def project(left, right):
    flat = left.reshape(-1, left.shape[-1])
    result = jnp.dot(flat, right, precision=highest, preferred_element_type=jnp.float32)
    return result.reshape(left.shape[:-1] + (right.shape[-1],))

def rms_scale(hidden, gain):
    return hidden * lax.rsqrt(lax.optimization_barrier(jnp.mean(hidden * hidden, axis=-1, keepdims=True)) + epsilon) * gain

def relative_bias(table, length, causal):
    bucket = bucket_matrix(length, causal)
    labels = jnp.arange(BUCKETS, dtype=jnp.int32)
    onehot = (bucket[:, :, None] == labels).astype(jnp.float32).reshape(length * length, BUCKETS)
    return project(onehot, table).reshape(length, length, -1).transpose(2, 0, 1)

def attention(query, keys, values, bias, allowed):
    scale = HEAD ** (-0.5)

    def one_row(item):
        row_query, row_keys, row_values, row_allowed = item
        scores = jnp.einsum('qhe,khe->hqk', row_query, row_keys, precision=highest) * scale + bias
        scores = jnp.where(row_allowed[None], low_back(scores), masked_score)
        peak = lax.optimization_barrier(jnp.max(scores, axis=2, keepdims=True))
        exponent = jnp.exp(scores - peak)
        weights = exponent / lax.optimization_barrier(jnp.sum(exponent, axis=2, keepdims=True))
        return jnp.einsum('hqk,khe->qhe', low(weights), row_values, precision=highest)
    mixed = lax.map(jax.checkpoint(one_row), (query, keys, values, allowed))
    return both_ways(mixed.reshape(mixed.shape[:2] + (-1,)))

def self_block(hidden, gain, mixing, projecting, bias, allowed):
    rows, length = hidden.shape[:2]
    normed = low(rms_scale(hidden, gain))
    projected = both_ways(project(normed, mixing.reshape(mixing.shape[0], -1)))
    projected = projected.reshape(rows, length, 3, -1, HEAD)
    mixed = attention(projected[:, :, 0], projected[:, :, 1], projected[:, :, 2], bias, allowed)
    return hidden + low_back(project(mixed, projecting))

def dense_block(hidden, gain, expanding, contracting):
    normed = low(rms_scale(hidden, gain))
    activated = low(jax.nn.gelu(low_back(project(normed, expanding)), approximate=True))
    return hidden + low_back(project(activated, contracting))

def two_layers(params, encoder_in, decoder_in, segments):
    mixing, projecting, crossing, expanding, contracting, gains, tables = params
    rows, length = encoder_in.shape[:2]
    encoder_ids = segments[0]
    decoder_ids = segments[1]
    allowed = encoder_ids[:, :, None] == encoder_ids[:, None, :]
    hidden = self_block(encoder_in, gains[0, 0], mixing[0], projecting[0], relative_bias(tables[0], length, False), allowed)
    encoder_out = dense_block(hidden, gains[0, 1], expanding[0], contracting[0])
    memory = both_ways(project(low(rms_scale(encoder_out, gains[0, 2])), crossing[0].reshape(crossing.shape[1], -1)))
    memory = memory.reshape(rows, length, 2, -1, HEAD)
    order = jnp.arange(length, dtype=jnp.int32)
    causal = order[None, :] <= order[:, None]
    allowed_self = (decoder_ids[:, :, None] == decoder_ids[:, None, :]) & causal[None]
    hidden = self_block(decoder_in, gains[1, 0], mixing[1], projecting[1], relative_bias(tables[1], length, True), allowed_self)
    normed = low(rms_scale(hidden, gains[1, 1]))
    query = both_ways(project(normed, crossing[1, :, 0, :])).reshape(rows, length, -1, HEAD)
    allowed_cross = decoder_ids[:, :, None] == encoder_ids[:, None, :]
    mixed = attention(query, memory[:, :, 0], memory[:, :, 1], 0.0, allowed_cross)
    hidden = hidden + low_back(project(mixed, crossing[1, :, 1, :].T))
    decoder_out = dense_block(hidden, gains[1, 2], expanding[1], contracting[1])
    return (encoder_out, decoder_out)

def reference(layer_inputs, output_cotangents, segment_ids, attention_in, attention_out, cross_weights, expand_weights, contract_weights, norm_gains, bias_tables):
    params = (attention_in.astype(jnp.float32), attention_out.astype(jnp.float32), cross_weights.astype(jnp.float32), expand_weights.astype(jnp.float32), contract_weights.astype(jnp.float32), norm_gains.astype(jnp.float32), bias_tables.astype(jnp.float32))
    groups = N_DP
    group_rows = ROWS // groups
    inputs = layer_inputs.astype(jnp.float32).reshape(2, groups, group_rows, LEN, D).transpose(1, 0, 2, 3, 4)
    cotangents = output_cotangents.astype(jnp.float32).reshape(2, groups, group_rows, LEN, D).transpose(1, 0, 2, 3, 4)
    segments = segment_ids.reshape(2, groups, group_rows, LEN).transpose(1, 0, 2, 3)

    def group_step(totals, item):
        group_inputs, group_cotangents, group_segments = item

        def forward(weights, encoder_in, decoder_in):
            return two_layers(weights, encoder_in, decoder_in, group_segments)
        outputs, pullback = jax.vjp(forward, params, group_inputs[0], group_inputs[1])
        weight_grads, encoder_grad, decoder_grad = pullback((group_cotangents[0], group_cotangents[1]))
        totals = jax.tree.map(jnp.add, totals, weight_grads)
        return (totals, (jnp.stack([outputs[0], outputs[1]]), jnp.stack([encoder_grad, decoder_grad])))
    start = jax.tree.map(jnp.zeros_like, params)
    totals, (outputs, gradients) = lax.scan(group_step, start, (inputs, cotangents, segments))
    layer_outputs = outputs.transpose(1, 0, 2, 3, 4).reshape(2, ROWS, LEN, D)
    input_gradient = gradients.transpose(1, 0, 2, 3, 4).reshape(2, ROWS, LEN, D)
    return (layer_outputs, input_gradient, totals[0], totals[1], totals[2], totals[3], totals[4], totals[5], totals[6])
```

```python
import functools

import jax
import jax.numpy as jnp
import numpy as np
from jax import lax
from jax.experimental import pallas as pl
from jax.experimental.pallas import tpu as pltpu
from jax.sharding import Mesh
from jax.sharding import PartitionSpec as P

D = 1024
HEAD = 64
BUCKETS = 32
MAXDIST = 128


epsilon = 1e-06
masked_score = -1e30
highest = lax.Precision.HIGHEST
bf16 = jnp.bfloat16
f32 = jnp.float32


def dot_t(a, b):
    return lax.dot_general(a, b, (((1,), (1,)), ((), ())), preferred_element_type=f32)


def dot_n(a, b):
    return lax.dot_general(a, b, (((1,), (0,)), ((), ())), preferred_element_type=f32)


def t_dot(a, b):
    return lax.dot_general(a, b, (((0,), (0,)), ((), ())), preferred_element_type=f32)


def toeplitz(vector, length):
    wide = jnp.broadcast_to(vector, (length, 2 * length))
    return pltpu.roll(wide, length, 1, stride=1, stride_axis=0)[:, :length]


def diagonal_sums(block):
    length = block.shape[0]
    row = lax.broadcasted_iota(jnp.int32, (length, length), 0)
    column = lax.broadcasted_iota(jnp.int32, (length, length), 1)
    upside = dot_n((row + column == length - 1).astype(bf16), block)
    wide = jnp.concatenate([upside, jnp.zeros_like(upside)], axis=1)
    return jnp.sum(pltpu.roll(wide, 1, 1, stride=1, stride_axis=0), axis=0, keepdims=True)


def allowed_pairs(query_ids, key_ids, causal):
    allowed = query_ids == key_ids
    if causal:
        key = lax.broadcasted_iota(jnp.int32, allowed.shape, 1)
        query = lax.broadcasted_iota(jnp.int32, allowed.shape, 0)
        allowed = allowed & (key <= query)
    return allowed


def attend_kernel(causal, biased, q_ref, k_ref, v_ref, query_ids, key_ids, *rest):
    if biased:
        vector, out_ref, log_ref = rest
    else:
        out_ref, log_ref = rest
    q = q_ref[0] * bf16(HEAD**-0.5)
    k, v = k_ref[0], v_ref[0]
    lane = lax.broadcasted_iota(jnp.int32, (1, 2 * HEAD), 1)
    allowed = allowed_pairs(query_ids[0], key_ids[0], causal)
    out, logs = None, []
    for head in range(2):
        mine = (lane // HEAD) == head
        scores = dot_t(jnp.where(mine, q, jnp.zeros_like(q)), k)
        if biased:
            scores = scores + toeplitz(vector[0, head : head + 1], scores.shape[0])
        scores = jnp.where(allowed, scores, masked_score)
        peak = jnp.max(scores, axis=1, keepdims=True)
        exponent = jnp.exp(scores - peak)
        total = jnp.sum(exponent, axis=1, keepdims=True)
        weights = (exponent * (1.0 / total)).astype(bf16)
        mixed = dot_n(weights, v)
        out = mixed if out is None else jnp.where(mine, mixed, out)
        logs.append(peak + jnp.log(total))
    out_ref[...] = out.astype(bf16)
    log_ref[0, 0] = jnp.concatenate(logs, axis=1)


def attend_back_kernel(
    causal, biased, q_ref, k_ref, v_ref, query_ids, key_ids, up_ref, log_ref, *rest
):
    if biased:
        vector, dq_ref, dk_ref, dv_ref, diagonal_ref = rest
    else:
        dq_ref, dk_ref, dv_ref = rest
    q = q_ref[0] * bf16(HEAD**-0.5)
    k, v, up = k_ref[0], v_ref[0], up_ref[...]
    lane = lax.broadcasted_iota(jnp.int32, (1, 2 * HEAD), 1)
    allowed = allowed_pairs(query_ids[0], key_ids[0], causal)
    dq = dk = dv = None
    for head in range(2):
        mine = (lane // HEAD) == head
        own_q = jnp.where(mine, q, jnp.zeros_like(q))
        own_up = jnp.where(mine, up, jnp.zeros_like(up))
        scores = dot_t(own_q, k)
        if biased:
            scores = scores + toeplitz(vector[0, head : head + 1], scores.shape[0])
        scores = jnp.where(allowed, scores - log_ref[0, 0, :, head : head + 1], masked_score)
        weights = jnp.exp(scores)
        dots = dot_t(own_up, v)
        inner = jnp.sum(weights * dots, axis=1, keepdims=True)
        grad = (weights * (dots - inner)).astype(bf16)
        a, b, c = dot_n(grad, k), t_dot(grad, own_q), t_dot(weights.astype(bf16), own_up)
        dq = a if head == 0 else jnp.where(mine, a, dq)
        dk = b if head == 0 else dk + b
        dv = c if head == 0 else dv + c
        if biased:
            diagonal_ref[0, 0, head : head + 1] = diagonal_sums(grad)
    dq_ref[0] = (dq * (HEAD**-0.5)).astype(bf16)
    dk_ref[0] = dk.astype(bf16)
    dv_ref[0] = dv.astype(bf16)


little = pl.CostEstimate(flops=1, bytes_accessed=1, transcendentals=1)
kernel_params = pltpu.CompilerParams(vmem_limit_bytes=48 * 1024 * 1024)


def operand_specs(parts, length):
    def one(index):
        return pl.BlockSpec((1, length, 2 * HEAD), lambda r, p: (index, r, p))

    return [one(index) for index in parts] + [
        pl.BlockSpec((1, length, 1), lambda r, p: (r, 0, 0)),
        pl.BlockSpec((1, 1, length), lambda r, p: (r, 0, 0)),
    ]


def attend(query, stored, parts, query_ids, key_ids, vector, causal):
    rows, length = query_ids.shape
    width = query.shape[2]
    pairs = width // (2 * HEAD)
    biased = vector is not None
    specs, more = operand_specs(parts, length), ()
    if biased:
        specs.append(pl.BlockSpec((1, 2, 2 * length), lambda r, p: (p, 0, 0)))
        more = (vector.reshape(pairs, 2, 2 * length),)
    return pl.pallas_call(
        functools.partial(attend_kernel, causal, biased),
        grid=(rows, pairs),
        in_specs=specs,
        out_specs=[
            pl.BlockSpec((length, 2 * HEAD), lambda r, p: (r, p)),
            pl.BlockSpec((1, 1, length, 2), lambda r, p: (r, p, 0, 0)),
        ],
        out_shape=[
            jax.ShapeDtypeStruct((rows * length, width), bf16),
            jax.ShapeDtypeStruct((rows, pairs, length, 2), f32),
        ],
        compiler_params=kernel_params,
        cost_estimate=little,
    )(query, stored, stored, query_ids[:, :, None], key_ids[:, None, :], *more)


def attend_back(query, stored, parts, query_ids, key_ids, vector, causal, up, logs):
    rows, length = query_ids.shape
    width = query.shape[2]
    pairs = width // (2 * HEAD)
    biased = vector is not None
    each = pl.BlockSpec((1, length, 2 * HEAD), lambda r, p: (0, r, p))
    shape = jax.ShapeDtypeStruct((1, rows * length, width), bf16)
    specs = operand_specs(parts, length) + [
        pl.BlockSpec((length, 2 * HEAD), lambda r, p: (r, p)),
        pl.BlockSpec((1, 1, length, 2), lambda r, p: (r, p, 0, 0)),
    ]
    out_specs, out_shape, more = [each] * 3, [shape] * 3, ()
    if biased:
        specs.append(pl.BlockSpec((1, 2, 2 * length), lambda r, p: (p, 0, 0)))
        more = (vector.reshape(pairs, 2, 2 * length),)
        out_specs.append(pl.BlockSpec((1, 1, 2, 2 * length), lambda r, p: (r, p, 0, 0)))
        out_shape.append(jax.ShapeDtypeStruct((rows, pairs, 2, 2 * length), f32))
    return pl.pallas_call(
        functools.partial(attend_back_kernel, causal, biased),
        grid=(rows, pairs),
        in_specs=specs,
        out_specs=out_specs,
        out_shape=out_shape,
        compiler_params=kernel_params,
        cost_estimate=little,
    )(query, stored, stored, query_ids[:, :, None], key_ids[:, None, :], up, logs, *more)


def bucket_onehot(length, causal):
    count = BUCKETS if causal else BUCKETS // 2
    exact = count // 2
    distance = np.arange(length)
    spread = exact + (
        np.log(np.maximum(distance, 1) / exact) / np.log(MAXDIST / exact) * (count - exact)
    ).astype(np.int64)
    levels = np.where(distance < exact, distance, np.minimum(spread, count - 1))
    breaks = [
        int(np.argmax(levels >= level))
        for level in range(1, count)
        if bool((levels >= level).any())
    ]
    offset = np.arange(2 * length) - length
    if causal:
        reach = np.maximum(-offset, 0)
        bucket = np.zeros(2 * length, np.int64)
    else:
        reach = np.abs(offset)
        bucket = np.where(offset > 0, count, 0)
    for edge in breaks:
        bucket = bucket + (reach >= edge)
    return jnp.asarray(bucket[:, None] == np.arange(BUCKETS)[None, :], f32)


def swap_section(value):
    return lax.ppermute(value, "section", [(0, 1), (1, 0)])


def swap_tensor(value):
    return lax.ppermute(value, "tensor", [(0, 1), (1, 0)])


def ordered(index, mine, other, axis):
    return jnp.where(
        index == 0,
        jnp.concatenate([mine, other], axis=axis),
        jnp.concatenate([other, mine], axis=axis),
    )


def hold(value, *after):
    return lax.optimization_barrier((value, after))[0]


def joined_features(local, other, axis=1):
    if lax.axis_size("tensor") == 2:
        return ordered(lax.axis_index("tensor"), local, other, axis)
    return lax.all_gather(local, "tensor", axis=axis, tiled=True)


def gather_features(local, axis=1):
    return joined_features(local, swap_tensor(local) if lax.axis_size("tensor") == 2 else local, axis)


def own_features(full):
    count = lax.axis_size("tensor")
    width = full.shape[1] // count
    return lax.dynamic_slice_in_dim(full, lax.axis_index("tensor") * width, width, 1)


def total_features(low):
    if lax.axis_size("tensor") == 2:
        return low.astype(f32) + swap_tensor(low).astype(f32)
    return lax.psum(low, "tensor").astype(f32)


def scatter_features(low):
    if lax.axis_size("tensor") == 2:
        width = low.shape[1] // 2
        first = lax.axis_index("tensor") == 0
        left, right = low[:, :width], low[:, width:]
        received = swap_tensor(jnp.where(first, right, left))
        return jnp.where(first, left, right).astype(f32) + received.astype(f32)
    return lax.psum_scatter(low, "tensor", scatter_dimension=1, tiled=True).astype(f32)


def total_tokens(values):
    if lax.axis_size("tensor") == 2:
        return values + swap_tensor(values.reshape(-1, 128)).reshape(-1)
    return lax.psum(values, "tensor")


def smooth(values):
    return jax.nn.gelu(values, approximate=True)


def matmul(a, b):
    return jnp.dot(a, b, preferred_element_type=f32)


def matmul_t(a, b):
    return jnp.einsum("tc,dc->td", a, b, preferred_element_type=f32)


def weight_grad(a, b):
    return jnp.einsum("tc,td->cd", a, b, preferred_element_type=f32).astype(bf16)


def norm_forward(hidden, gain):
    inverse = lax.rsqrt(jnp.mean(hidden * hidden, axis=1, keepdims=True) + epsilon)
    return ((hidden * inverse * gain).astype(bf16), inverse)


def norm_backward(hidden, gain, inverse, upstream):
    scaled = upstream * gain
    inner = jnp.sum(scaled * hidden, axis=1, keepdims=True)
    return inverse * scaled - hidden * (inverse * inverse * inverse * inner / D)


def gain_gradient(hidden, inverse, upstream):
    return jnp.sum(upstream * hidden * inverse, axis=0)


def self_forward(hidden, gain, mixing, projecting, vector, ids, causal):
    normed, inverse = norm_forward(hidden, gain)
    projected = jnp.einsum("td,edc->etc", normed, mixing, preferred_element_type=f32).astype(bf16)
    mixed, logs = attend(projected, projected, (0, 1, 2), ids, ids, vector, causal)
    return (matmul(mixed, projecting).astype(bf16), (normed, inverse, projected, mixed, logs))


def self_backward(projecting, vector, ids, causal, kept, low):
    normed, inverse, projected, mixed, logs = kept
    up = matmul_t(low, projecting).astype(bf16)
    dq, dk, dv, diagonals = attend_back(
        projected, projected, (0, 1, 2), ids, ids, vector, causal, up, logs
    )
    return ((dq[0], dk[0], dv[0]), diagonals)


def mixing_back(parts, mixing):
    return sum(matmul_t(part, mixing[index]) for index, part in enumerate(parts)).astype(bf16)


def input_gradient_of(hidden, gain, inverse, partial_value, grad):
    inner = total_tokens(jnp.sum(partial_value.astype(f32) * gain * hidden, axis=1))[:, None]
    upstream = scatter_features(partial_value)
    own, own_gain = own_features(hidden), own_features(gain[None])
    result = inverse * upstream * own_gain - own * (inverse * inverse * inverse * inner / D)
    return (result + own_features(grad), gain_gradient(own, inverse, upstream))


def dense_forward(hidden, gain, expanding, contracting):
    normed, inverse = norm_forward(hidden, gain)
    before = matmul(normed, expanding)
    activated = smooth(before).astype(bf16)
    return (activated, (normed, inverse, before, activated))


def dense_backward(expanding, contracting, kept, low):
    normed, inverse, before, activated = kept
    upward = matmul_t(low, contracting)
    again, smooth_back = jax.vjp(smooth, before)
    before_grad = smooth_back(upward)[0].astype(bf16)
    return (before_grad, matmul_t(before_grad, expanding).astype(bf16))


def section_half(value):
    half = value.shape[0] // 2
    first = lax.axis_index("section") == 0
    received = swap_section(jnp.where(first, value[half:], value[:half]))
    return jnp.where(first, value[:half], value[half:]) + received


def section_own(encoder_value, decoder_value):
    first = lax.axis_index("section") == 0
    received = swap_section(jnp.where(first, decoder_value, encoder_value))
    return jnp.where(first, encoder_value, decoder_value) + received


def sum_rows(values):
    return lax.psum(values, ("z", "y"))


def sum_rows_small(value):
    if lax.axis_size("z") != 4 or lax.axis_size("y") != 2:
        return lax.psum(value, ("z", "y"))
    value = value.reshape(-1, 128)
    value = value + lax.ppermute(value, "y", [(0, 1), (1, 0)])
    value = value + lax.ppermute(value, "z", [(i, i ^ 1) for i in range(4)])
    return value + lax.ppermute(value, "z", [(i, i ^ 2) for i in range(4)])


ring = [2 * z for z in range(4)] + [2 * z + 1 for z in reversed(range(4))]


def along_ring(value, way):
    pairs = [(ring[i], ring[(i + way) % 8]) for i in range(8)]
    return lax.ppermute(value, ("z", "y"), pairs)


def ring_pieces(groups):
    z, y = lax.axis_index("z"), lax.axis_index("y")
    place = jnp.where(y == 0, z, 7 - z)
    ways = (1, -1)

    def piece(value, index):
        return lax.dynamic_index_in_dim(value, lax.rem(index + 16, 8), 0, keepdims=False)

    def put(value, part, index):
        return lax.dynamic_update_index_in_dim(value, part, lax.rem(index + 16, 8), 0)

    return place, ways, piece, put


def ring_start(groups):
    place, ways, piece, put = ring_pieces(groups)
    moving = [[piece(value, place) for value in pair] for pair in groups]
    return ring_step(groups, moving, 0)


def ring_step(groups, moving, step):
    place, ways, piece, put = ring_pieces(groups)
    moving = list(moving)
    for g, pair in enumerate(groups):
        received = [along_ring(moving[g][w], ways[w]) for w in range(2)]
        moving[g] = [
            received[w] + piece(pair[w], place - ways[w] * (step + 1)) for w in range(2)
        ]
    return moving


def ring_finish(groups, moving):
    place, ways, piece, put = ring_pieces(groups)
    for step in range(1, 7):
        moving = ring_step(groups, moving, step)
    totals = [
        [put(pair[w], moving[g][w], place + ways[w]) for w in range(2)]
        for g, pair in enumerate(groups)
    ]
    for step in range(7):
        for g, pair in enumerate(totals):
            moving[g] = [along_ring(moving[g][w], ways[w]) for w in range(2)]
            totals[g] = [
                put(totals[g][w], moving[g][w], place - ways[w] * step) for w in range(2)
            ]
        if step == 4:
            late = moving
    return (totals, late)


def body(
    layer_inputs,
    output_cotangents,
    segment_ids,
    attention_in,
    attention_out,
    cross_weights,
    expand_weights,
    contract_weights,
    norm_gains,
    bias_tables,
):
    all_rows, length, local_width = layer_inputs.shape[1:]
    rows = all_rows // 2
    tokens = rows * length
    section = lax.axis_index("section")
    first = section == 0

    def pick(mine, other):
        return (jnp.where(first, mine, other), jnp.where(first, other, mine))

    def both(mine, *after):
        return pick(mine, swap_section(hold(mine, *after)))

    def own_rows(value):
        mine = lax.dynamic_slice_in_dim(value[0], section * rows, rows, 0)
        give = lax.dynamic_slice_in_dim(value[0], (1 - section) * rows, rows, 0)
        return pick(mine.reshape(tokens, -1), swap_section(give).reshape(tokens, -1))

    def all_layer_rows(encoder_value, decoder_value):
        mine = jnp.where(first, encoder_value, decoder_value)
        other = swap_section(jnp.where(first, decoder_value, encoder_value))
        return ordered(section, mine, other, 0).reshape(1, all_rows, length, local_width)

    encoder_half, decoder_half = own_rows(layer_inputs)
    mixing = both(attention_in[0].transpose(1, 0, 2))
    encoder_in = gather_features(encoder_half).astype(f32)
    own_gains = gather_features(norm_gains[0])
    small_own = jnp.concatenate([own_gains.reshape(-1), bias_tables[0].reshape(-1)])
    small_both = both(small_own)
    gains = [part[: own_gains.size].reshape(own_gains.shape) for part in small_both]
    tables = [part[own_gains.size :].reshape(bias_tables.shape[1:]) for part in small_both]
    projecting, expanding, contracting, crossing = lax.all_gather(
        (attention_out[0], expand_weights[0], contract_weights[0], cross_weights[0].transpose(1, 0, 2)),
        "section",
    )
    encoder_cotangent, decoder_cotangent = own_rows(output_cotangents)
    later_halves = hold(jnp.stack([decoder_half, encoder_cotangent, decoder_cotangent]), encoder_in)
    later_others = swap_tensor(later_halves) if lax.axis_size("tensor") == 2 else later_halves
    encoder_in = hold(encoder_in, mixing)
    ids = lax.dynamic_slice_in_dim(segment_ids, section * rows, rows, 1)
    encoder_ids, decoder_ids = ids[0], ids[1]
    onehots = (bucket_onehot(length, False), bucket_onehot(length, True))
    vectors = [
        jnp.einsum("bh,jb->hj", table, onehot, precision=highest)
        for table, onehot in zip(tables, onehots)
    ]

    x1_part, encoder_self = self_forward(
        encoder_in, gains[0][0], mixing[0], projecting[0], vectors[0], encoder_ids, False
    )
    later_halves, later_others = hold((later_halves, later_others), x1_part)
    decoder_in, encoder_cotangent, decoder_cotangent = joined_features(later_halves, later_others, 2)
    decoder_in = decoder_in.astype(f32)
    z1_part, decoder_self = self_forward(
        decoder_in, gains[1][0], mixing[1], projecting[1], vectors[1], decoder_ids, True
    )
    x1 = encoder_in + total_features(x1_part)
    activated, encoder_dense = dense_forward(hold(x1, z1_part), gains[0][1], expanding[0], contracting[0])
    x2_part = matmul(activated, contracting[0]).astype(bf16)
    z1 = decoder_in + total_features(z1_part)
    cross_in, cross_inverse = norm_forward(z1, gains[1][1])
    query = matmul(cross_in, crossing[1][0]).astype(bf16)[None]
    x2 = x1 + total_features(x2_part)
    memory_in, memory_inverse = norm_forward(x2, gains[0][2])
    memory = jnp.einsum("td,edc->etc", memory_in, crossing[0], preferred_element_type=f32)
    memory = memory.astype(bf16)
    cross_mixed, cross_logs = attend(
        query, memory, (0, 0, 1), decoder_ids, encoder_ids, None, False
    )
    z2_part = matmul_t(cross_mixed, crossing[1][1]).astype(bf16)
    z2 = z1 + total_features(z2_part)
    activated, decoder_dense = dense_forward(z2, gains[1][2], expanding[1], contracting[1])

    before_grad, part = dense_backward(expanding[1], contracting[1], decoder_dense, decoder_cotangent)
    upstream = total_features(part)
    activated, before_grad, normed = hold((activated, before_grad, decoder_dense[0]), part)
    decoder_contract = weight_grad(activated, decoder_cotangent)
    decoder_expand = weight_grad(normed, before_grad)
    upstream = hold(upstream, decoder_contract, decoder_expand)
    first_halves = [section_half(decoder_contract), section_half(decoder_expand)]
    first_sums = sum_rows(first_halves)
    dz2 = norm_backward(z2, gains[1][2], decoder_dense[1], upstream) + decoder_cotangent.astype(f32)
    gain_two = gain_gradient(z2, decoder_dense[1], upstream)

    low = dz2.astype(bf16)
    up = matmul(hold(low, first_halves), crossing[1][1]).astype(bf16)
    dquery, dkeys, dvalues = attend_back(
        query, memory, (0, 0, 1), decoder_ids, encoder_ids, None, False, up, cross_logs
    )
    memory_part = sum(
        matmul_t(part[0], crossing[0][index]) for index, part in enumerate((dkeys, dvalues))
    ).astype(bf16)
    memory_up = total_features(memory_part)
    dquery, dkeys, dvalues, low = hold((dquery, dkeys, dvalues, low), memory_part)
    query_part = matmul_t(dquery[0], crossing[1][0]).astype(bf16)
    decoder_cross = jnp.stack([weight_grad(cross_in, dquery[0]), weight_grad(low, cross_mixed)])
    encoder_cross = jnp.stack(
        [weight_grad(memory_in, dkeys[0]), weight_grad(memory_in, dvalues[0])]
    )

    memory_up, decoder_cross, encoder_cross = lax.optimization_barrier(
        (memory_up, decoder_cross, encoder_cross)
    )

    dx2 = norm_backward(x2, gains[0][2], memory_inverse, memory_up) + encoder_cotangent.astype(f32)
    query_up = total_features(hold(query_part, memory_up))
    low = dx2.astype(bf16)
    before_grad, part = dense_backward(expanding[0], contracting[0], encoder_dense, low)
    upstream = total_features(part)

    before_grad, activated, normed, low, query_up = hold(
        (before_grad, encoder_dense[3], encoder_dense[0], low, query_up), part
    )
    encoder_contract = weight_grad(activated, low)
    encoder_expand = weight_grad(normed, before_grad)
    query_up = hold(query_up, encoder_contract, encoder_expand)
    dz1 = norm_backward(z1, gains[1][1], cross_inverse, query_up) + dz2
    decoder_low = dz1.astype(bf16)
    decoder_dqkv, decoder_diagonals = self_backward(
        projecting[1], vectors[1], decoder_ids, True, decoder_self, decoder_low
    )

    upstream = hold(upstream, decoder_dqkv)
    dx1 = norm_backward(x1, gains[0][1], encoder_dense[1], upstream) + dx2
    low = dx1.astype(bf16)
    encoder_dqkv, encoder_diagonals = self_backward(
        projecting[0], vectors[0], encoder_ids, False, encoder_self, low
    )

    decoder_dqkv, decoder_low, low = hold((decoder_dqkv, decoder_low, low), encoder_dqkv)
    encoder_mixing = jnp.stack([weight_grad(encoder_self[0], value) for value in encoder_dqkv])
    decoder_mixing = jnp.stack([weight_grad(decoder_self[0], value) for value in decoder_dqkv])
    encoder_projecting = weight_grad(encoder_self[3], low)
    decoder_projecting = weight_grad(decoder_self[3], decoder_low)

    encoder_dqkv, decoder_dqkv, activated = hold(
        (encoder_dqkv, decoder_dqkv, decoder_dense[3]),
        encoder_mixing, decoder_mixing, encoder_projecting, decoder_projecting,
    )
    encoder_part = mixing_back(encoder_dqkv, mixing[0])
    decoder_part = mixing_back(decoder_dqkv, mixing[1])
    out_part = matmul(activated, contracting[1]).astype(bf16)

    def narrowed(value, width):
        return jnp.concatenate(
            [value[:, at : at + width] for at in range(0, value.shape[1], width)], axis=0
        )

    def widened(value, width):
        count = width // value.shape[1]
        length = value.shape[0] // count
        return jnp.concatenate(
            [value[at * length : (at + 1) * length] for at in range(count)], axis=1
        )

    contract_sum = section_half(encoder_contract)
    expand_sum = section_half(encoder_expand)
    mixing_sum = section_own(encoder_mixing, decoder_mixing)
    projecting_sum = section_own(encoder_projecting, decoder_projecting)

    narrow = mixing_sum.shape[2]
    groups, encoder_part, decoder_part, out_part = lax.optimization_barrier((
        [
            [contract_sum, expand_sum],
            [
                mixing_sum[:2].reshape(-1, narrow),
                jnp.concatenate([mixing_sum[2], narrowed(projecting_sum, narrow)]),
            ],
        ],
        encoder_part, decoder_part, out_part,
    ))
    first_sums = hold(first_sums, groups)
    cross_sum = section_own(encoder_cross, decoder_cross)
    cross_sum = sum_rows(hold(cross_sum, first_sums))
    groups = [[value.reshape(8, -1, value.shape[1]) for value in pair] for pair in groups]
    whole_ring = lax.axis_size("z") == 4 and lax.axis_size("y") == 2
    moving = ring_start(groups) if whole_ring else groups

    encoder_part, decoder_part, out_part, memory_up, upstream = hold(
        (encoder_part, decoder_part, out_part, memory_up, upstream), moving
    )
    encoder_gain_two = gain_gradient(x2, memory_inverse, memory_up)
    encoder_gain_one = gain_gradient(x1, encoder_dense[1], upstream)
    gain_one = gain_gradient(z1, cross_inverse, query_up)
    encoder_grad, encoder_gain_zero = input_gradient_of(
        encoder_in, gains[0][0], encoder_self[1], encoder_part, dx1
    )
    decoder_grad, gain_zero = input_gradient_of(
        decoder_in, gains[1][0], decoder_self[1], decoder_part, dz1
    )
    decoder_out = own_features(z2) + scatter_features(out_part)

    def small(gain_zero, gain_one, gain_two, diagonals, onehot):
        ones = [gain_zero[None], own_features(gain_one[None]), own_features(gain_two[None])]
        summed = jnp.sum(diagonals, axis=0).reshape(-1, 2 * length)
        table = jnp.einsum("hj,jb->bh", summed, onehot, precision=highest)
        return jnp.concatenate(ones + [table.reshape(1, -1)], axis=1)

    decoder_small = small(gain_zero, gain_one, gain_two, decoder_diagonals, onehots[1])
    encoder_small = small(
        encoder_gain_zero, encoder_gain_one, encoder_gain_two, encoder_diagonals, onehots[0]
    )
    small_sum = sum_rows_small(section_own(encoder_small, decoder_small))
    if whole_ring:
        totals, late = ring_finish(groups, moving)
    else:
        totals = late = sum_rows(groups)
    (contract_sum, expand_sum), (query_key_sum, last) = [
        [value.reshape(-1, value.shape[2]) for value in pair] for pair in totals
    ]
    mixing_sum = jnp.concatenate([query_key_sum, last[:D]]).reshape(3, D, narrow)
    projecting_sum = widened(last[D:], D)
    cross_sum = hold(cross_sum, late)
    small_sum = small_sum.reshape(-1)

    def whole(encoder_sum, decoder_sum):
        mine = jnp.where(first, encoder_sum, decoder_sum)
        other = swap_section(jnp.where(first, decoder_sum, encoder_sum))
        return ordered(section, mine, other, 0).astype(f32)

    width = D // lax.axis_size("tensor")
    return (
        all_layer_rows(own_features(x2), decoder_out),
        all_layer_rows(encoder_grad, decoder_grad),
        mixing_sum.astype(f32).transpose(1, 0, 2)[None],
        projecting_sum.astype(f32)[None],
        cross_sum.astype(f32).transpose(1, 0, 2)[None],
        whole(expand_sum, first_sums[1])[None],
        whole(contract_sum, first_sums[0])[None],
        small_sum[: 3 * width].reshape(1, 3, width),
        small_sum[3 * width :].reshape(1, BUCKETS, -1),
    )


def solution(mesh):
    sections, groups, width = mesh.devices.shape
    along = 4 if groups % 4 == 0 else groups
    mesh = Mesh(
        mesh.devices.reshape(sections, along, groups // along, width),
        ("section", "z", "y", "tensor"),
    )
    return jax.shard_map(
        body,
        mesh=mesh,
        in_specs=(
            P("section", ("z", "y"), None, "tensor"),
            P("section", ("z", "y"), None, "tensor"),
            P(None, ("z", "y"), None),
            P("section", None, None, "tensor"),
            P("section", "tensor", None),
            P("section", None, None, "tensor"),
            P("section", None, "tensor"),
            P("section", "tensor", None),
            P("section", None, "tensor"),
            P("section", None, "tensor"),
        ),
        out_specs=(
            P("section", ("z", "y"), None, "tensor"),
            P("section", ("z", "y"), None, "tensor"),
            P("section", None, None, "tensor"),
            P("section", "tensor", None),
            P("section", None, None, "tensor"),
            P("section", None, "tensor"),
            P("section", "tensor", None),
            P("section", None, "tensor"),
            P("section", None, "tensor"),
        ),
        check_vma=False,
    )
```

```python
import functools

import jax
import jax.numpy as jnp
import numpy as np
from jax import lax
from jax.experimental import pallas as pl
from jax.experimental.pallas import tpu as pltpu
from jax.sharding import Mesh
from jax.sharding import PartitionSpec as P

D = 1024
HEAD = 64
BUCKETS = 32
MAXDIST = 128


epsilon = 1e-06
masked_score = -1e30
highest = lax.Precision.HIGHEST
bf16 = jnp.bfloat16
f32 = jnp.float32


def dot_t(a, b):
    return lax.dot_general(a, b, (((1,), (1,)), ((), ())), preferred_element_type=f32)


def dot_n(a, b):
    return lax.dot_general(a, b, (((1,), (0,)), ((), ())), preferred_element_type=f32)


def t_dot(a, b):
    return lax.dot_general(a, b, (((0,), (0,)), ((), ())), preferred_element_type=f32)


def toeplitz(vector, start, rows, count):
    length = vector.shape[1] // 2
    near = vector[:, length - start - rows : length - start + count]
    wide = jnp.broadcast_to(near, (rows, rows + count))
    return pltpu.roll(wide, count, 1, stride=1, stride_axis=0)[:, :count]


def diagonal_sums(block):
    length = block.shape[0]
    row = lax.broadcasted_iota(jnp.int32, (length, length), 0)
    column = lax.broadcasted_iota(jnp.int32, (length, length), 1)
    upside = dot_n((row + column == length - 1).astype(bf16), block)
    wide = jnp.concatenate([upside, jnp.zeros_like(upside)], axis=1)
    return jnp.sum(pltpu.roll(wide, 1, 1, stride=1, stride_axis=0), axis=0, keepdims=True)


def attend_kernel(causal, biased, q_ref, k_ref, v_ref, query_ids, key_ids, *rest):
    if biased:
        vector, out_ref, log_ref = rest
    else:
        out_ref, log_ref = rest
    lane = lax.broadcasted_iota(jnp.int32, (1, 2 * HEAD), 1)
    length = q_ref.shape[1]
    rows = min(256, length) if biased else length
    for start in range(0, length, rows):
        count = start + rows if causal else length
        block = slice(start, start + rows)
        q = q_ref[0, block] * bf16(HEAD**-0.5)
        k, v = k_ref[0, :count], v_ref[0, :count]
        allowed = query_ids[0, block] == key_ids[0, :, :count]
        if causal:
            key = lax.broadcasted_iota(jnp.int32, allowed.shape, 1)
            query = lax.broadcasted_iota(jnp.int32, allowed.shape, 0) + start
            allowed = allowed & (key <= query)
        out, logs = None, []
        for head in range(2):
            mine = (lane // HEAD) == head
            scores = dot_t(jnp.where(mine, q, jnp.zeros_like(q)), k)
            if biased:
                scores = scores + toeplitz(vector[0, head : head + 1], start, rows, count)
            scores = jnp.where(allowed, scores, masked_score)
            peak = jnp.max(scores, axis=1, keepdims=True)
            exponent = jnp.exp(scores - peak)
            total = jnp.sum(exponent, axis=1, keepdims=True)
            weights = (exponent * (1.0 / total)).astype(bf16)
            mixed = dot_n(weights, v)
            out = mixed if out is None else jnp.where(mine, mixed, out)
            logs.append(peak + jnp.log(total))
        out_ref[block] = out.astype(bf16)
        log_ref[0, 0, block] = jnp.concatenate(logs, axis=1)


def attend_back_kernel(
    causal, biased, q_ref, k_ref, v_ref, query_ids, key_ids, up_ref, log_ref, *rest
):
    if biased:
        vector, dq_ref, dk_ref, dv_ref, diagonal_ref = rest
    else:
        dq_ref, dk_ref, dv_ref = rest
    q = q_ref[0] * bf16(HEAD**-0.5)
    k, v, up = k_ref[0], v_ref[0], up_ref[...]
    lane = lax.broadcasted_iota(jnp.int32, (1, 2 * HEAD), 1)
    allowed = key_ids[0] == query_ids[0]
    if causal:
        key = lax.broadcasted_iota(jnp.int32, allowed.shape, 0)
        query = lax.broadcasted_iota(jnp.int32, allowed.shape, 1)
        allowed = allowed & (key <= query)
    dq = dk = dv = None
    for head in range(2):
        mine = (lane // HEAD) == head
        own_q = jnp.where(mine, q, jnp.zeros_like(q))
        own_up = jnp.where(mine, up, jnp.zeros_like(up))
        scores = dot_t(k, own_q)
        if biased:
            size = scores.shape[0]
            scores = scores + toeplitz(vector[0, head : head + 1], 0, size, size)
        scores = jnp.where(allowed, scores - log_ref[0, 0, head : head + 1, :], masked_score)
        weights = jnp.exp(scores)
        dots = dot_t(v, own_up)
        inner = jnp.sum(weights * dots, axis=0, keepdims=True)
        grad = (weights * (dots - inner)).astype(bf16)
        a, b, c = t_dot(grad, k), dot_n(grad, own_q), dot_n(weights.astype(bf16), own_up)
        dq = a if head == 0 else jnp.where(mine, a, dq)
        dk = b if head == 0 else dk + b
        dv = c if head == 0 else dv + c
        if biased:
            diagonal_ref[0, 0, head : head + 1] = diagonal_sums(grad)
    dq_ref[0] = (dq * (HEAD**-0.5)).astype(bf16)
    dk_ref[0] = dk.astype(bf16)
    dv_ref[0] = dv.astype(bf16)


def turned(vector):
    return jnp.roll(jnp.flip(vector, axis=-1), 1, axis=-1)


little = pl.CostEstimate(flops=1, bytes_accessed=1, transcendentals=1)
kernel_params = pltpu.CompilerParams(vmem_limit_bytes=48 * 1024 * 1024)


def operand_specs(parts, length):
    def one(index):
        return pl.BlockSpec((1, length, 2 * HEAD), lambda r, p: (index, r, p))

    return [one(index) for index in parts] + [
        pl.BlockSpec((1, length, 1), lambda r, p: (r, 0, 0)),
        pl.BlockSpec((1, 1, length), lambda r, p: (r, 0, 0)),
    ]


def attend(query, stored, parts, query_ids, key_ids, vector, causal):
    rows, length = query_ids.shape
    width = query.shape[2]
    pairs = width // (2 * HEAD)
    biased = vector is not None
    specs, more = operand_specs(parts, length), ()
    if biased:
        specs.append(pl.BlockSpec((1, 2, 2 * length), lambda r, p: (p, 0, 0)))
        more = (vector.reshape(pairs, 2, 2 * length),)
    mixed, logs = pl.pallas_call(
        functools.partial(attend_kernel, causal, biased),
        grid=(rows, pairs),
        in_specs=specs,
        out_specs=[
            pl.BlockSpec((length, 2 * HEAD), lambda r, p: (r, p)),
            pl.BlockSpec((1, 1, length, 2), lambda r, p: (r, p, 0, 0)),
        ],
        out_shape=[
            jax.ShapeDtypeStruct((rows * length, width), bf16),
            jax.ShapeDtypeStruct((rows, pairs, length, 2), f32),
        ],
        compiler_params=kernel_params,
        cost_estimate=little,
    )(query, stored, stored, query_ids[:, :, None], key_ids[:, None, :], *more)
    return (mixed, logs.swapaxes(2, 3))


def attend_back(query, stored, parts, query_ids, key_ids, vector, causal, up, logs):
    rows, length = query_ids.shape
    width = query.shape[2]
    pairs = width // (2 * HEAD)
    biased = vector is not None
    each = pl.BlockSpec((1, length, 2 * HEAD), lambda r, p: (0, r, p))
    shape = jax.ShapeDtypeStruct((1, rows * length, width), bf16)
    specs = operand_specs(parts, length)[:3] + [
        pl.BlockSpec((1, 1, length), lambda r, p: (r, 0, 0)),
        pl.BlockSpec((1, length, 1), lambda r, p: (r, 0, 0)),
        pl.BlockSpec((length, 2 * HEAD), lambda r, p: (r, p)),
        pl.BlockSpec((1, 1, 2, length), lambda r, p: (r, p, 0, 0)),
    ]
    out_specs, out_shape, more = [each] * 3, [shape] * 3, ()
    if biased:
        specs.append(pl.BlockSpec((1, 2, 2 * length), lambda r, p: (p, 0, 0)))
        more = (turned(vector).reshape(pairs, 2, 2 * length),)
        out_specs.append(pl.BlockSpec((1, 1, 2, 2 * length), lambda r, p: (r, p, 0, 0)))
        out_shape.append(jax.ShapeDtypeStruct((rows, pairs, 2, 2 * length), f32))
    result = pl.pallas_call(
        functools.partial(attend_back_kernel, causal, biased),
        grid=(rows, pairs),
        in_specs=specs,
        out_specs=out_specs,
        out_shape=out_shape,
        compiler_params=kernel_params,
        cost_estimate=little,
    )(query, stored, stored, query_ids[:, None, :], key_ids[:, :, None], up, logs, *more)
    return list(result[:3]) + [turned(part) for part in result[3:]]


def bucket_onehot(length, causal):
    count = BUCKETS if causal else BUCKETS // 2
    exact = count // 2
    distance = np.arange(length)
    spread = exact + (
        np.log(np.maximum(distance, 1) / exact) / np.log(MAXDIST / exact) * (count - exact)
    ).astype(np.int64)
    levels = np.where(distance < exact, distance, np.minimum(spread, count - 1))
    breaks = [
        int(np.argmax(levels >= level))
        for level in range(1, count)
        if bool((levels >= level).any())
    ]
    offset = np.arange(2 * length) - length
    if causal:
        reach = np.maximum(-offset, 0)
        bucket = np.zeros(2 * length, np.int64)
    else:
        reach = np.abs(offset)
        bucket = np.where(offset > 0, count, 0)
    for edge in breaks:
        bucket = bucket + (reach >= edge)
    return jnp.asarray(bucket[:, None] == np.arange(BUCKETS)[None, :], f32)


def swap_section(value):
    return lax.ppermute(value, "section", [(0, 1), (1, 0)])


def swap_tensor(value):
    return lax.ppermute(value, "tensor", [(0, 1), (1, 0)])


def ordered(index, mine, other, axis):
    return jnp.where(
        index == 0,
        jnp.concatenate([mine, other], axis=axis),
        jnp.concatenate([other, mine], axis=axis),
    )


def hold(value, *after):
    return lax.optimization_barrier((value, after))[0]


def joined_features(local, other, axis=1):
    if lax.axis_size("tensor") == 2:
        return ordered(lax.axis_index("tensor"), local, other, axis)
    return lax.all_gather(local, "tensor", axis=axis, tiled=True)


def gather_features(local, axis=1):
    return joined_features(local, swap_tensor(local) if lax.axis_size("tensor") == 2 else local, axis)


def own_features(full):
    count = lax.axis_size("tensor")
    width = full.shape[1] // count
    return lax.dynamic_slice_in_dim(full, lax.axis_index("tensor") * width, width, 1)


def exchange(low):
    if lax.axis_size("tensor") == 2:
        return (low, swap_tensor(low))
    return (lax.psum(low, "tensor"), jnp.zeros_like(low))


def total(parts):
    return parts[0].astype(f32) + parts[1].astype(f32)


def total_features(low):
    return total(exchange(low))


def scatter_begin(lows):
    if lax.axis_size("tensor") == 2:
        width = lows[0].shape[1] // 2
        first = lax.axis_index("tensor") == 0
        give = jnp.stack([jnp.where(first, low[:, width:], low[:, :width]) for low in lows])
        keep = [jnp.where(first, low[:, :width], low[:, width:]) for low in lows]
        return (keep, swap_tensor(give))
    return (
        [lax.psum_scatter(low, "tensor", scatter_dimension=1, tiled=True) for low in lows],
        None,
    )


def scatter_end(kept, received):
    if received is None:
        return [part.astype(f32) for part in kept]
    return [part.astype(f32) + received[index].astype(f32) for index, part in enumerate(kept)]


def total_begin(values):
    if lax.axis_size("tensor") == 2:
        return (values, swap_tensor(values.reshape(-1, 128)))
    return (lax.psum(values, "tensor"), None)


def total_end(values, received):
    return values if received is None else values + received.reshape(values.shape)


def smooth(values):
    return jax.nn.gelu(values, approximate=True)


def matmul(a, b):
    return jnp.dot(a, b, preferred_element_type=f32)


def matmul_t(a, b):
    return jnp.einsum("tc,dc->td", a, b, preferred_element_type=f32)


def weight_grad(a, b):
    return jnp.einsum("tc,td->cd", a, b, preferred_element_type=f32).astype(bf16)


def norm_forward(hidden, gain):
    inverse = lax.rsqrt(jnp.mean(hidden * hidden, axis=1, keepdims=True) + epsilon)
    return ((hidden * inverse * gain).astype(bf16), inverse)


def norm_backward(hidden, gain, inverse, upstream):
    scaled = upstream * gain
    inner = jnp.sum(scaled * hidden, axis=1, keepdims=True)
    return inverse * scaled - hidden * (inverse * inverse * inverse * inner / D)


def gain_gradient(hidden, inverse, upstream):
    return jnp.sum(upstream * hidden * inverse, axis=0)


def self_forward(hidden, gain, mixing, projecting, vector, ids, causal):
    normed, inverse = norm_forward(hidden, gain)
    projected = jnp.einsum("td,edc->etc", normed, mixing, preferred_element_type=f32).astype(bf16)
    mixed, logs = attend(projected, projected, (0, 1, 2), ids, ids, vector, causal)
    return (matmul(mixed, projecting).astype(bf16), (normed, inverse, projected, mixed, logs))


def self_backward(projecting, vector, ids, causal, kept, low):
    normed, inverse, projected, mixed, logs = kept
    up = matmul_t(low, projecting).astype(bf16)
    dq, dk, dv, diagonals = attend_back(
        projected, projected, (0, 1, 2), ids, ids, vector, causal, up, logs
    )
    return ((dq[0], dk[0], dv[0]), diagonals)


def mixing_back(parts, mixing):
    return sum(matmul_t(part, mixing[index]) for index, part in enumerate(parts)).astype(bf16)


def input_gradient_of(hidden, gain, inverse, upstream, inner, grad):
    own, own_gain = own_features(hidden), own_features(gain[None])
    result = inverse * upstream * own_gain
    result = result - own * (inverse * inverse * inverse * inner[:, None] / D)
    return (result + own_features(grad), gain_gradient(own, inverse, upstream))


def dense_forward(hidden, gain, expanding, contracting):
    normed, inverse = norm_forward(hidden, gain)
    before = matmul(normed, expanding)
    activated = smooth(before).astype(bf16)
    return (activated, (normed, inverse, before, activated))


def dense_backward(expanding, contracting, kept, low):
    normed, inverse, before, activated = kept
    upward = matmul_t(low, contracting)
    again, smooth_back = jax.vjp(smooth, before)
    before_grad = smooth_back(upward)[0].astype(bf16)
    return (before_grad, matmul_t(before_grad, expanding).astype(bf16))


def weight_own(encoder_pair, decoder_pair):
    first = lax.axis_index("section") == 0
    keep = [jnp.where(first, e, d) for e, d in zip(encoder_pair, decoder_pair)]
    give = [jnp.where(first, d, e) for e, d in zip(encoder_pair, decoder_pair)]
    received = swap_section(weight_grad(*give))
    total = jnp.einsum("tc,td->cd", *keep, preferred_element_type=f32) + received.astype(f32)
    return total.astype(bf16)


def section_half(value):
    half = value.shape[0] // 2
    first = lax.axis_index("section") == 0
    received = swap_section(jnp.where(first, value[half:], value[:half]))
    return jnp.where(first, value[:half], value[half:]) + received


def section_own(encoder_value, decoder_value):
    first = lax.axis_index("section") == 0
    received = swap_section(jnp.where(first, decoder_value, encoder_value))
    return jnp.where(first, encoder_value, decoder_value) + received


def sum_rows(values):
    return lax.psum(values, ("z", "y"))


def swap_y(value):
    return lax.ppermute(value, "y", [(0, 1), (1, 0)])


def swap_z(value, distance):
    return lax.ppermute(value, "z", [(i, i ^ distance) for i in range(4)])


ring = [2 * z for z in range(4)] + [2 * z + 1 for z in reversed(range(4))]


def along_ring(value, way):
    pairs = [(ring[i], ring[(i + way) % 8]) for i in range(8)]
    return lax.ppermute(value, ("z", "y"), pairs)


class RingSum:

    ways = (1, -1)

    def __init__(self, groups):
        self.groups, self.count = groups, 0
        self.around = lax.axis_size("z") == 4 and lax.axis_size("y") == 2
        z, y = lax.axis_index("z"), lax.axis_index("y")
        self.place = jnp.where(y == 0, z, 7 - z)
        if self.around:
            self.moving = [[self.piece(v, self.place) for v in pair] for pair in groups]

    def piece(self, value, index):
        return lax.dynamic_index_in_dim(value, lax.rem(index + 16, 8), 0, keepdims=False)

    def put(self, value, part, index):
        return lax.dynamic_update_index_in_dim(value, part, lax.rem(index + 16, 8), 0)

    def step(self, group=0):
        if not self.around:
            return ()
        place, ways, step = self.place, self.ways, self.count % 7
        if self.count == 7:
            self.totals = [
                [self.put(v, m, place + way) for v, m, way in zip(pair, moving, ways)]
                for pair, moving in zip(self.groups, self.moving)
            ]
        self.moving = [
            [along_ring(m, way) for m, way in zip(moving, ways)] for moving in self.moving
        ]
        if self.count < 7:
            self.moving = [
                [
                    m + self.piece(v, place - way * (step + 1))
                    for v, m, way in zip(pair, moving, ways)
                ]
                for pair, moving in zip(self.groups, self.moving)
            ]
        else:
            self.totals = [
                [self.put(t, m, place - way * step) for t, m, way in zip(pair, moving, ways)]
                for pair, moving in zip(self.totals, self.moving)
            ]
        self.count += 1
        return self.moving[group]

    def sums(self):
        if not self.around:
            return sum_rows(self.groups)
        while self.count < 14:
            self.step()
        return self.totals


def body(
    layer_inputs,
    output_cotangents,
    segment_ids,
    attention_in,
    attention_out,
    cross_weights,
    expand_weights,
    contract_weights,
    norm_gains,
    bias_tables,
):
    all_rows, length, local_width = layer_inputs.shape[1:]
    rows = all_rows // 2
    tokens = rows * length
    section = lax.axis_index("section")
    first = section == 0

    def pick(mine, other):
        return (jnp.where(first, mine, other), jnp.where(first, other, mine))

    def both(mine, *after):
        return pick(mine, swap_section(hold(mine, *after)))

    def own_rows(value):
        mine = lax.dynamic_slice_in_dim(value[0], section * rows, rows, 0)
        give = lax.dynamic_slice_in_dim(value[0], (1 - section) * rows, rows, 0)
        return pick(mine.reshape(tokens, -1), swap_section(give).reshape(tokens, -1))

    encoder_half, decoder_half = own_rows(layer_inputs)
    mixing = both(attention_in[0].transpose(1, 0, 2))
    encoder_in = gather_features(encoder_half).astype(f32)
    own_gains = gather_features(norm_gains[0])
    small_own = jnp.concatenate([own_gains.reshape(-1), bias_tables[0].reshape(-1)])
    small_both = both(small_own)
    gains = [part[: own_gains.size].reshape(own_gains.shape) for part in small_both]
    tables = [part[own_gains.size :].reshape(bias_tables.shape[1:]) for part in small_both]
    projecting, expanding, contracting, crossing = lax.all_gather(
        (attention_out[0], expand_weights[0], contract_weights[0], cross_weights[0].transpose(1, 0, 2)),
        "section",
    )
    encoder_cotangent, decoder_cotangent = own_rows(output_cotangents)
    decoder_halves = hold(jnp.stack([decoder_half, decoder_cotangent]), encoder_in)
    decoder_others = swap_tensor(decoder_halves) if lax.axis_size("tensor") == 2 else decoder_halves
    encoder_in = hold(encoder_in, mixing)
    ids = lax.dynamic_slice_in_dim(segment_ids, section * rows, rows, 1)
    encoder_ids, decoder_ids = ids[0], ids[1]
    onehots = (bucket_onehot(length, False), bucket_onehot(length, True))
    vectors = [
        jnp.einsum("bh,jb->hj", table, onehot, precision=highest)
        for table, onehot in zip(tables, onehots)
    ]

    x1_part, encoder_self = self_forward(
        encoder_in, gains[0][0], mixing[0], projecting[0], vectors[0], encoder_ids, False
    )
    decoder_halves, decoder_others = hold((decoder_halves, decoder_others), x1_part)
    decoder_in, decoder_cotangent = joined_features(decoder_halves, decoder_others, 2)
    decoder_in = decoder_in.astype(f32)
    z1_part, decoder_self = self_forward(
        decoder_in, gains[1][0], mixing[1], projecting[1], vectors[1], decoder_ids, True
    )
    x1 = encoder_in + total_features(x1_part)
    activated, encoder_dense = dense_forward(hold(x1, z1_part), gains[0][1], expanding[0], contracting[0])
    x2_part = matmul(activated, contracting[0]).astype(bf16)
    z1 = decoder_in + total_features(z1_part)
    cross_in, cross_inverse = norm_forward(z1, gains[1][1])
    query = matmul(cross_in, crossing[1][0]).astype(bf16)[None]
    x2 = x1 + total_features(x2_part)
    encoder_cotangent = gather_features(hold(encoder_cotangent, x2))
    memory_in, memory_inverse = norm_forward(x2, gains[0][2])
    memory = jnp.einsum("td,edc->etc", memory_in, crossing[0], preferred_element_type=f32)
    memory = memory.astype(bf16)
    cross_mixed, cross_logs = attend(
        query, memory, (0, 0, 1), decoder_ids, encoder_ids, None, False
    )
    z2_part = matmul_t(cross_mixed, crossing[1][1]).astype(bf16)
    z2_part, encoder_cotangent = lax.optimization_barrier((z2_part, encoder_cotangent))
    z2 = z1 + total_features(z2_part)
    activated, decoder_dense = dense_forward(z2, gains[1][2], expanding[1], contracting[1])

    before_grad, part = dense_backward(expanding[1], contracting[1], decoder_dense, decoder_cotangent)
    upstream = total_features(part)
    activated, before_grad, normed = hold((activated, before_grad, decoder_dense[0]), part)
    decoder_contract = weight_grad(activated, decoder_cotangent)
    decoder_expand = weight_grad(normed, before_grad)
    upstream = hold(upstream, decoder_contract, decoder_expand)
    first_halves = [section_half(decoder_contract), section_half(decoder_expand)]
    first_sums = sum_rows(first_halves)
    dz2 = norm_backward(z2, gains[1][2], decoder_dense[1], upstream) + decoder_cotangent.astype(f32)
    gain_two = gain_gradient(z2, decoder_dense[1], upstream)

    low = dz2.astype(bf16)
    up = matmul(hold(low, first_halves), crossing[1][1]).astype(bf16)
    dquery, dkeys, dvalues = attend_back(
        query, memory, (0, 0, 1), decoder_ids, encoder_ids, None, False, up, cross_logs
    )
    memory_part = sum(
        matmul_t(part[0], crossing[0][index]) for index, part in enumerate((dkeys, dvalues))
    ).astype(bf16)
    memory_up = total_features(memory_part)
    dquery, dkeys, dvalues, low = hold((dquery, dkeys, dvalues, low), memory_part)
    query_part = matmul_t(dquery[0], crossing[1][0]).astype(bf16)
    decoder_cross = jnp.stack([weight_grad(cross_in, dquery[0]), weight_grad(low, cross_mixed)])
    encoder_cross = jnp.stack(
        [weight_grad(memory_in, dkeys[0]), weight_grad(memory_in, dvalues[0])]
    )

    cross_sum = section_own(encoder_cross, decoder_cross)
    memory_up, decoder_cross, encoder_cross = lax.optimization_barrier(
        (memory_up, decoder_cross, encoder_cross)
    )

    dx2 = norm_backward(x2, gains[0][2], memory_inverse, memory_up) + encoder_cotangent.astype(f32)
    query_own, query_other = exchange(hold(query_part, memory_up))
    low = dx2.astype(bf16)
    before_grad, part = dense_backward(expanding[0], contracting[0], encoder_dense, low)
    upstream = total_features(part)

    before_grad, activated, normed, low, query_own = hold(
        (before_grad, encoder_dense[3], encoder_dense[0], low, query_own), part
    )
    encoder_contract = weight_grad(activated, low)
    encoder_expand = weight_grad(normed, before_grad)
    query_own = hold(query_own, encoder_contract, encoder_expand)
    query_up = total((query_own, query_other))
    dz1 = norm_backward(z1, gains[1][1], cross_inverse, query_up) + dz2
    decoder_low = dz1.astype(bf16)
    decoder_dqkv, decoder_diagonals = self_backward(
        projecting[1], vectors[1], decoder_ids, True, decoder_self, decoder_low
    )

    upstream = hold(upstream, decoder_dqkv)
    dx1 = norm_backward(x1, gains[0][1], encoder_dense[1], upstream) + dx2
    low = dx1.astype(bf16)
    encoder_dqkv, encoder_diagonals = self_backward(
        projecting[0], vectors[0], encoder_ids, False, encoder_self, low
    )

    decoder_dqkv, decoder_low, low = hold((decoder_dqkv, decoder_low, low), encoder_dqkv)
    mixing_sum = [
        weight_own((encoder_self[0], e), (decoder_self[0], d))
        for e, d in zip(encoder_dqkv, decoder_dqkv)
    ]
    projecting_sum = weight_own((encoder_self[3], low), (decoder_self[3], decoder_low))

    encoder_dqkv, decoder_dqkv = hold((encoder_dqkv, decoder_dqkv), mixing_sum, projecting_sum)
    out_part = matmul(decoder_dense[3], contracting[1]).astype(bf16)
    encoder_part = mixing_back(encoder_dqkv, mixing[0])
    decoder_part = mixing_back(decoder_dqkv, mixing[1])

    def narrowed(value, width):
        return jnp.concatenate(
            [value[:, at : at + width] for at in range(0, value.shape[1], width)], axis=0
        )

    def widened(value, width):
        count = width // value.shape[1]
        length = value.shape[0] // count
        return jnp.concatenate(
            [value[at * length : (at + 1) * length] for at in range(count)], axis=1
        )

    contract_sum = section_half(encoder_contract)
    expand_sum = section_half(encoder_expand)
    mixing_sum = jnp.stack(mixing_sum)

    narrow = mixing_sum.shape[2]
    inners = jnp.stack(
        [
            jnp.sum(part.astype(f32) * gain[0] * hidden, axis=1)
            for part, gain, hidden in zip(
                (encoder_part, decoder_part), gains, (encoder_in, decoder_in)
            )
        ]
    )
    kept, received = scatter_begin((encoder_part, decoder_part, out_part))
    inners, other_inners = total_begin(inners)
    groups, kept, inners = lax.optimization_barrier(
        (
            [
                [contract_sum, expand_sum],
                [
                    mixing_sum[:2].reshape(-1, narrow),
                    jnp.concatenate([mixing_sum[2], narrowed(projecting_sum, narrow)]),
                ],
            ],
            kept,
            inners,
        )
    )
    first_sums = hold(first_sums, groups)
    cross_sum = sum_rows(hold(cross_sum, first_sums))
    ring_sum = RingSum(
        [[value.reshape(8, -1, value.shape[1]) for value in pair] for pair in groups]
    )
    ring_sum.step()
    ring_sum.step()
    now = ring_sum.step()

    received, other_inners = hold((received, other_inners), now)
    inners = total_end(inners, other_inners)
    encoder_up, decoder_up, out_sum = scatter_end(kept, received)
    encoder_gain_two = gain_gradient(x2, memory_inverse, memory_up)
    encoder_gain_one = gain_gradient(x1, encoder_dense[1], upstream)
    gain_one = gain_gradient(z1, cross_inverse, query_up)
    encoder_grad, encoder_gain_zero = input_gradient_of(
        encoder_in, gains[0][0], encoder_self[1], encoder_up, inners[0], dx1
    )
    decoder_grad, gain_zero = input_gradient_of(
        decoder_in, gains[1][0], decoder_self[1], decoder_up, inners[1], dz1
    )
    decoder_out = own_features(z2) + out_sum

    def small(gain_zero, gain_one, gain_two, diagonals, onehot):
        ones = [gain_zero[None], own_features(gain_one[None]), own_features(gain_two[None])]
        summed = jnp.sum(diagonals, axis=0).reshape(-1, 2 * length)
        table = jnp.einsum("hj,jb->bh", summed, onehot, precision=highest)
        return jnp.concatenate(ones + [table.reshape(1, -1)], axis=1)

    small_sum = section_own(
        small(
            encoder_gain_zero, encoder_gain_one, encoder_gain_two, encoder_diagonals, onehots[0]
        ),
        small(gain_zero, gain_one, gain_two, decoder_diagonals, onehots[1]),
    )
    mine, give = pick(
        jnp.stack([own_features(x2), encoder_grad]), jnp.stack([decoder_out, decoder_grad])
    )
    other = swap_section(give)
    ring_sum.step()
    ring_sum.step()
    now = ring_sum.step()
    layer_outputs, input_gradient = ordered(section, mine, hold(other, now), 1).reshape(
        2, 1, all_rows, length, local_width
    )
    if ring_sum.around:
        small_sum = small_sum.reshape(-1, 128)
        small_sum = small_sum + hold(swap_y(hold(small_sum, now)), ring_sum.step())
        ring_sum.step()
        small_sum = small_sum + hold(swap_z(small_sum, 1), ring_sum.step())
        ring_sum.step()
        small_sum = small_sum + hold(swap_z(small_sum, 2), ring_sum.step())
        small_sum = small_sum.reshape(-1)
    else:
        small_sum = sum_rows(small_sum).reshape(-1)
    late = ring_sum.step()
    (contract_sum, expand_sum), (query_key_sum, last) = [
        [value.reshape(-1, value.shape[2]) for value in pair] for pair in ring_sum.sums()
    ]
    mixing_sum = jnp.concatenate([query_key_sum, last[:D]]).reshape(3, D, narrow)
    projecting_sum = widened(last[D:], D)
    cross_sum = hold(cross_sum, late)

    def whole(encoder_sum, decoder_sum):
        mine = jnp.where(first, encoder_sum, decoder_sum)
        other = swap_section(jnp.where(first, decoder_sum, encoder_sum))
        return ordered(section, mine, other, 0).astype(f32)

    width = D // lax.axis_size("tensor")
    return (
        layer_outputs,
        input_gradient,
        mixing_sum.astype(f32).transpose(1, 0, 2)[None],
        projecting_sum.astype(f32)[None],
        cross_sum.astype(f32).transpose(1, 0, 2)[None],
        whole(expand_sum, first_sums[1])[None],
        whole(contract_sum, first_sums[0])[None],
        small_sum[: 3 * width].reshape(1, 3, width),
        small_sum[3 * width :].reshape(1, BUCKETS, -1),
    )


def solution(mesh):
    sections, groups, width = mesh.devices.shape
    along = 4 if groups % 4 == 0 else groups
    mesh = Mesh(
        mesh.devices.reshape(sections, along, groups // along, width),
        ("section", "z", "y", "tensor"),
    )
    return jax.shard_map(
        body,
        mesh=mesh,
        in_specs=(
            P("section", ("z", "y"), None, "tensor"),
            P("section", ("z", "y"), None, "tensor"),
            P(None, ("z", "y"), None),
            P("section", None, None, "tensor"),
            P("section", "tensor", None),
            P("section", None, None, "tensor"),
            P("section", None, "tensor"),
            P("section", "tensor", None),
            P("section", None, "tensor"),
            P("section", None, "tensor"),
        ),
        out_specs=(
            P("section", ("z", "y"), None, "tensor"),
            P("section", ("z", "y"), None, "tensor"),
            P("section", None, None, "tensor"),
            P("section", "tensor", None),
            P("section", None, None, "tensor"),
            P("section", None, "tensor"),
            P("section", "tensor", None),
            P("section", None, "tensor"),
            P("section", None, "tensor"),
        ),
        check_vma=False,
    )
```

```python
import functools

import jax
import jax.numpy as jnp
import numpy as np
from jax import lax
from jax.experimental import pallas as pl
from jax.experimental.pallas import tpu as pltpu
from jax.sharding import Mesh
from jax.sharding import PartitionSpec as P

D = 1024
HEAD = 64
BUCKETS = 32
MAXDIST = 128


epsilon = 1e-06
masked_score = -1e30
highest = lax.Precision.HIGHEST
bf16 = jnp.bfloat16
f32 = jnp.float32


def dot_t(a, b):
    return lax.dot_general(a, b, (((1,), (1,)), ((), ())), preferred_element_type=f32)


def dot_n(a, b):
    return lax.dot_general(a, b, (((1,), (0,)), ((), ())), preferred_element_type=f32)


def t_dot(a, b):
    return lax.dot_general(a, b, (((0,), (0,)), ((), ())), preferred_element_type=f32)


def toeplitz(vector, start, rows, count):
    length = vector.shape[1] // 2
    near = vector[:, length - start - rows : length - start + count]
    wide = jnp.broadcast_to(near, (rows, rows + count))
    return pltpu.roll(wide, count, 1, stride=1, stride_axis=0)[:, :count]


def diagonal_sums(block):
    length = block.shape[0]
    row = lax.broadcasted_iota(jnp.int32, (length, length), 0)
    column = lax.broadcasted_iota(jnp.int32, (length, length), 1)
    upside = dot_n((row + column == length - 1).astype(bf16), block)
    wide = jnp.concatenate([upside, jnp.zeros_like(upside)], axis=1)
    return jnp.sum(pltpu.roll(wide, 1, 1, stride=1, stride_axis=0), axis=0, keepdims=True)


def attend_kernel(causal, biased, q_ref, k_ref, v_ref, query_ids, key_ids, *rest):
    if biased:
        vector, out_ref, log_ref = rest
    else:
        out_ref, log_ref = rest
    lane = lax.broadcasted_iota(jnp.int32, (1, 2 * HEAD), 1)
    length = q_ref.shape[1]
    rows = min(256, length) if biased else length
    for start in range(0, length, rows):
        count = start + rows if causal else length
        block = slice(start, start + rows)
        q = q_ref[0, block] * bf16(HEAD**-0.5)
        k, v = k_ref[0, :count], v_ref[0, :count]
        allowed = query_ids[0, block] == key_ids[0, :, :count]
        if causal:
            key = lax.broadcasted_iota(jnp.int32, allowed.shape, 1)
            query = lax.broadcasted_iota(jnp.int32, allowed.shape, 0) + start
            allowed = allowed & (key <= query)
        out, logs = None, []
        for head in range(2):
            mine = (lane // HEAD) == head
            scores = dot_t(jnp.where(mine, q, jnp.zeros_like(q)), k)
            if biased:
                scores = scores + toeplitz(vector[0, head : head + 1], start, rows, count)
            scores = jnp.where(allowed, scores, masked_score)
            peak = jnp.max(scores, axis=1, keepdims=True)
            exponent = jnp.exp(scores - peak)
            total = jnp.sum(exponent, axis=1, keepdims=True)
            weights = (exponent * (1.0 / total)).astype(bf16)
            mixed = dot_n(weights, v)
            out = mixed if out is None else jnp.where(mine, mixed, out)
            logs.append(peak + jnp.log(total))
        out_ref[block] = out.astype(bf16)
        log_ref[0, 0, block] = jnp.concatenate(logs, axis=1)


def attend_back_kernel(
    causal, biased, q_ref, k_ref, v_ref, query_ids, key_ids, up_ref, log_ref, *rest
):
    if biased:
        vector, dq_ref, dk_ref, dv_ref, diagonal_ref = rest
    else:
        dq_ref, dk_ref, dv_ref = rest
    q = q_ref[0] * bf16(HEAD**-0.5)
    k, v, up = k_ref[0], v_ref[0], up_ref[...]
    lane = lax.broadcasted_iota(jnp.int32, (1, 2 * HEAD), 1)
    allowed = key_ids[0] == query_ids[0]
    if causal:
        key = lax.broadcasted_iota(jnp.int32, allowed.shape, 0)
        query = lax.broadcasted_iota(jnp.int32, allowed.shape, 1)
        allowed = allowed & (key <= query)
    dq = dk = dv = None
    for head in range(2):
        mine = (lane // HEAD) == head
        own_q = jnp.where(mine, q, jnp.zeros_like(q))
        own_up = jnp.where(mine, up, jnp.zeros_like(up))
        scores = dot_t(k, own_q)
        if biased:
            size = scores.shape[0]
            scores = scores + toeplitz(vector[0, head : head + 1], 0, size, size)
        scores = jnp.where(allowed, scores - log_ref[0, 0, head : head + 1, :], masked_score)
        weights = jnp.exp(scores)
        dots = dot_t(v, own_up)
        inner = jnp.sum(weights * dots, axis=0, keepdims=True)
        grad = (weights * (dots - inner)).astype(bf16)
        a, b, c = t_dot(grad, k), dot_n(grad, own_q), dot_n(weights.astype(bf16), own_up)
        dq = a if head == 0 else jnp.where(mine, a, dq)
        dk = b if head == 0 else dk + b
        dv = c if head == 0 else dv + c
        if biased:
            diagonal_ref[0, 0, head : head + 1] = diagonal_sums(grad)
    dq_ref[0] = (dq * (HEAD**-0.5)).astype(bf16)
    dk_ref[0] = dk.astype(bf16)
    dv_ref[0] = dv.astype(bf16)


def turned(vector):
    return jnp.roll(jnp.flip(vector, axis=-1), 1, axis=-1)


little = pl.CostEstimate(flops=12_000_000_000, bytes_accessed=30_000_000, transcendentals=4_000_000)
kernel_params = pltpu.CompilerParams(vmem_limit_bytes=48 * 1024 * 1024)


def operand_specs(parts, length):
    def one(index):
        return pl.BlockSpec((1, length, 2 * HEAD), lambda r, p: (index, r, p))

    return [one(index) for index in parts] + [
        pl.BlockSpec((1, length, 1), lambda r, p: (r, 0, 0)),
        pl.BlockSpec((1, 1, length), lambda r, p: (r, 0, 0)),
    ]


def attend(query, stored, parts, query_ids, key_ids, vector, causal):
    rows, length = query_ids.shape
    width = query.shape[2]
    pairs = width // (2 * HEAD)
    biased = vector is not None
    specs, more = operand_specs(parts, length), ()
    if biased:
        specs.append(pl.BlockSpec((1, 2, 2 * length), lambda r, p: (p, 0, 0)))
        more = (vector.reshape(pairs, 2, 2 * length),)
    mixed, logs = pl.pallas_call(
        functools.partial(attend_kernel, causal, biased),
        grid=(rows, pairs),
        in_specs=specs,
        out_specs=[
            pl.BlockSpec((length, 2 * HEAD), lambda r, p: (r, p)),
            pl.BlockSpec((1, 1, length, 2), lambda r, p: (r, p, 0, 0)),
        ],
        out_shape=[
            jax.ShapeDtypeStruct((rows * length, width), bf16),
            jax.ShapeDtypeStruct((rows, pairs, length, 2), f32),
        ],
        compiler_params=kernel_params,
        cost_estimate=little,
    )(query, stored, stored, query_ids[:, :, None], key_ids[:, None, :], *more)
    return (mixed, logs.swapaxes(2, 3))


def attend_back(query, stored, parts, query_ids, key_ids, vector, causal, up, logs):
    rows, length = query_ids.shape
    width = query.shape[2]
    pairs = width // (2 * HEAD)
    biased = vector is not None
    each = pl.BlockSpec((1, length, 2 * HEAD), lambda r, p: (0, r, p))
    shape = jax.ShapeDtypeStruct((1, rows * length, width), bf16)
    specs = operand_specs(parts, length)[:3] + [
        pl.BlockSpec((1, 1, length), lambda r, p: (r, 0, 0)),
        pl.BlockSpec((1, length, 1), lambda r, p: (r, 0, 0)),
        pl.BlockSpec((length, 2 * HEAD), lambda r, p: (r, p)),
        pl.BlockSpec((1, 1, 2, length), lambda r, p: (r, p, 0, 0)),
    ]
    out_specs, out_shape, more = [each] * 3, [shape] * 3, ()
    if biased:
        specs.append(pl.BlockSpec((1, 2, 2 * length), lambda r, p: (p, 0, 0)))
        more = (turned(vector).reshape(pairs, 2, 2 * length),)
        out_specs.append(pl.BlockSpec((1, 1, 2, 2 * length), lambda r, p: (r, p, 0, 0)))
        out_shape.append(jax.ShapeDtypeStruct((rows, pairs, 2, 2 * length), f32))
    result = pl.pallas_call(
        functools.partial(attend_back_kernel, causal, biased),
        grid=(rows, pairs),
        in_specs=specs,
        out_specs=out_specs,
        out_shape=out_shape,
        compiler_params=kernel_params,
        cost_estimate=little,
    )(query, stored, stored, query_ids[:, None, :], key_ids[:, :, None], up, logs, *more)
    return list(result[:3]) + [turned(part) for part in result[3:]]


def bucket_onehot(length, causal):
    count = BUCKETS if causal else BUCKETS // 2
    exact = count // 2
    distance = np.arange(length)
    spread = exact + (
        np.log(np.maximum(distance, 1) / exact) / np.log(MAXDIST / exact) * (count - exact)
    ).astype(np.int64)
    levels = np.where(distance < exact, distance, np.minimum(spread, count - 1))
    breaks = [
        int(np.argmax(levels >= level))
        for level in range(1, count)
        if bool((levels >= level).any())
    ]
    offset = np.arange(2 * length) - length
    if causal:
        reach = np.maximum(-offset, 0)
        bucket = np.zeros(2 * length, np.int64)
    else:
        reach = np.abs(offset)
        bucket = np.where(offset > 0, count, 0)
    for edge in breaks:
        bucket = bucket + (reach >= edge)
    return jnp.asarray(bucket[:, None] == np.arange(BUCKETS)[None, :], f32)


def swap_section(value):
    return lax.ppermute(value, "section", [(0, 1), (1, 0)])


def swap_tensor(value):
    return lax.ppermute(value, "tensor", [(0, 1), (1, 0)])


def ordered(index, mine, other, axis):
    return jnp.where(
        index == 0,
        jnp.concatenate([mine, other], axis=axis),
        jnp.concatenate([other, mine], axis=axis),
    )


def hold(value, *after):
    return lax.optimization_barrier((value, after))[0]


def joined_features(local, other, axis=1):
    if lax.axis_size("tensor") == 2:
        return ordered(lax.axis_index("tensor"), local, other, axis)
    return lax.all_gather(local, "tensor", axis=axis, tiled=True)


def gather_features(local, axis=1):
    return joined_features(local, swap_tensor(local) if lax.axis_size("tensor") == 2 else local, axis)


def own_features(full):
    count = lax.axis_size("tensor")
    width = full.shape[1] // count
    return lax.dynamic_slice_in_dim(full, lax.axis_index("tensor") * width, width, 1)


def exchange(low):
    if lax.axis_size("tensor") == 2:
        return (low, swap_tensor(low))
    return (lax.psum(low, "tensor"), jnp.zeros_like(low))


def total(parts):
    return parts[0].astype(f32) + parts[1].astype(f32)


def total_features(low):
    return total(exchange(low))


def scatter_begin(lows):
    if lax.axis_size("tensor") == 2:
        width = lows[0].shape[1] // 2
        first = lax.axis_index("tensor") == 0
        give = jnp.stack([jnp.where(first, low[:, width:], low[:, :width]) for low in lows])
        keep = [jnp.where(first, low[:, :width], low[:, width:]) for low in lows]
        return (keep, swap_tensor(give))
    return (
        [lax.psum_scatter(low, "tensor", scatter_dimension=1, tiled=True) for low in lows],
        None,
    )


def scatter_end(kept, received):
    if received is None:
        return [part.astype(f32) for part in kept]
    return [part.astype(f32) + received[index].astype(f32) for index, part in enumerate(kept)]


def total_begin(values):
    if lax.axis_size("tensor") == 2:
        return (values, swap_tensor(values.reshape(-1, 128)))
    return (lax.psum(values, "tensor"), None)


def total_end(values, received):
    return values if received is None else values + received.reshape(values.shape)


def smooth(values):
    return jax.nn.gelu(values, approximate=True)


def matmul(a, b):
    return jnp.dot(a, b, preferred_element_type=f32)


def matmul_t(a, b):
    return jnp.einsum("tc,dc->td", a, b, preferred_element_type=f32)


def weight_grad(a, b):
    return jnp.einsum("tc,td->cd", a, b, preferred_element_type=f32).astype(bf16)


def norm_forward(hidden, gain):
    inverse = lax.rsqrt(jnp.mean(hidden * hidden, axis=1, keepdims=True) + epsilon)
    return ((hidden * inverse * gain).astype(bf16), inverse)


def norm_backward(hidden, gain, inverse, upstream):
    scaled = upstream * gain
    inner = jnp.sum(scaled * hidden, axis=1, keepdims=True)
    return inverse * scaled - hidden * (inverse * inverse * inverse * inner / D)


def gain_gradient(hidden, inverse, upstream):
    return jnp.sum(upstream * hidden * inverse, axis=0)


def self_forward(hidden, gain, mixing, projecting, vector, ids, causal):
    normed, inverse = norm_forward(hidden, gain)
    projected = jnp.einsum("td,edc->etc", normed, mixing, preferred_element_type=f32).astype(bf16)
    mixed, logs = attend(projected, projected, (0, 1, 2), ids, ids, vector, causal)
    return (matmul(mixed, projecting).astype(bf16), (normed, inverse, projected, mixed, logs))


def self_backward(projecting, vector, ids, causal, kept, low):
    normed, inverse, projected, mixed, logs = kept
    up = matmul_t(low, projecting).astype(bf16)
    dq, dk, dv, diagonals = attend_back(
        projected, projected, (0, 1, 2), ids, ids, vector, causal, up, logs
    )
    return ((dq[0], dk[0], dv[0]), diagonals)


def mixing_back(parts, mixing):
    return sum(matmul_t(part, mixing[index]) for index, part in enumerate(parts)).astype(bf16)


def input_gradient_of(hidden, gain, inverse, upstream, inner, grad):
    own, own_gain = own_features(hidden), own_features(gain[None])
    result = inverse * upstream * own_gain
    result = result - own * (inverse * inverse * inverse * inner[:, None] / D)
    return (result + own_features(grad), gain_gradient(own, inverse, upstream))


def dense_forward(hidden, gain, expanding, contracting):
    normed, inverse = norm_forward(hidden, gain)
    before = matmul(normed, expanding)
    activated = smooth(before).astype(bf16)
    return (activated, (normed, inverse, before, activated))


def dense_backward(expanding, contracting, kept, low):
    normed, inverse, before, activated = kept
    upward = matmul_t(low, contracting)
    again, smooth_back = jax.vjp(smooth, before)
    before_grad = smooth_back(upward)[0].astype(bf16)
    return (before_grad, matmul_t(before_grad, expanding).astype(bf16))


def weight_own(encoder_pair, decoder_pair):
    first = lax.axis_index("section") == 0
    keep = [jnp.where(first, e, d) for e, d in zip(encoder_pair, decoder_pair)]
    give = [jnp.where(first, d, e) for e, d in zip(encoder_pair, decoder_pair)]
    received = swap_section(weight_grad(*give))
    total = jnp.einsum("tc,td->cd", *keep, preferred_element_type=f32) + received.astype(f32)
    return total.astype(bf16)


def section_half(value):
    half = value.shape[0] // 2
    first = lax.axis_index("section") == 0
    received = swap_section(jnp.where(first, value[half:], value[:half]))
    return jnp.where(first, value[:half], value[half:]) + received


def section_own(encoder_value, decoder_value):
    first = lax.axis_index("section") == 0
    received = swap_section(jnp.where(first, decoder_value, encoder_value))
    return jnp.where(first, encoder_value, decoder_value) + received


def sum_rows(values):
    return lax.psum(values, ("z", "y"))


def swap_y(value):
    return lax.ppermute(value, "y", [(0, 1), (1, 0)])


def swap_z(value, distance):
    return lax.ppermute(value, "z", [(i, i ^ distance) for i in range(4)])


ring = [2 * z for z in range(4)] + [2 * z + 1 for z in reversed(range(4))]


def along_ring(value, way):
    pairs = [(ring[i], ring[(i + way) % 8]) for i in range(8)]
    return lax.ppermute(value, ("z", "y"), pairs)


class RingSum:

    ways = (1, -1)

    def __init__(self, groups):
        self.groups, self.count = groups, 0
        self.around = lax.axis_size("z") == 4 and lax.axis_size("y") == 2
        z, y = lax.axis_index("z"), lax.axis_index("y")
        self.place = jnp.where(y == 0, z, 7 - z)
        if self.around:
            self.moving = [[self.piece(v, self.place) for v in pair] for pair in groups]

    def piece(self, value, index):
        return lax.dynamic_index_in_dim(value, lax.rem(index + 16, 8), 0, keepdims=False)

    def put(self, value, part, index):
        return lax.dynamic_update_index_in_dim(value, part, lax.rem(index + 16, 8), 0)

    def step(self, group=0):
        if not self.around:
            return ()
        place, ways, step = self.place, self.ways, self.count % 7
        if self.count == 7:
            self.totals = [
                [self.put(v, m, place + way) for v, m, way in zip(pair, moving, ways)]
                for pair, moving in zip(self.groups, self.moving)
            ]
        self.moving = [
            [along_ring(m, way) for m, way in zip(moving, ways)] for moving in self.moving
        ]
        if self.count < 7:
            self.moving = [
                [
                    m + self.piece(v, place - way * (step + 1))
                    for v, m, way in zip(pair, moving, ways)
                ]
                for pair, moving in zip(self.groups, self.moving)
            ]
        else:
            self.totals = [
                [self.put(t, m, place - way * step) for t, m, way in zip(pair, moving, ways)]
                for pair, moving in zip(self.totals, self.moving)
            ]
        self.count += 1
        return self.moving[group]

    def sums(self):
        if not self.around:
            return sum_rows(self.groups)
        while self.count < 14:
            self.step()
        return self.totals


def body(
    layer_inputs,
    output_cotangents,
    segment_ids,
    attention_in,
    attention_out,
    cross_weights,
    expand_weights,
    contract_weights,
    norm_gains,
    bias_tables,
):
    all_rows, length, local_width = layer_inputs.shape[1:]
    rows = all_rows // 2
    tokens = rows * length
    section = lax.axis_index("section")
    first = section == 0

    def pick(mine, other):
        return (jnp.where(first, mine, other), jnp.where(first, other, mine))

    def both(mine, *after):
        return pick(mine, swap_section(hold(mine, *after)))

    def own_rows(value):
        mine = lax.dynamic_slice_in_dim(value[0], section * rows, rows, 0)
        give = lax.dynamic_slice_in_dim(value[0], (1 - section) * rows, rows, 0)
        return pick(mine.reshape(tokens, -1), swap_section(give).reshape(tokens, -1))

    encoder_half, decoder_half = own_rows(layer_inputs)
    mixing = lax.all_gather(attention_in[0].transpose(1, 0, 2), "section")
    encoder_in = gather_features(encoder_half).astype(f32)
    own_gains = gather_features(norm_gains[0])
    small_own = jnp.concatenate([own_gains.reshape(-1), bias_tables[0].reshape(-1)])
    small_both = both(small_own)
    gains = [part[: own_gains.size].reshape(own_gains.shape) for part in small_both]
    tables = [part[own_gains.size :].reshape(bias_tables.shape[1:]) for part in small_both]
    projecting, expanding, contracting, crossing = lax.all_gather(
        hold(
            (
                attention_out[0],
                expand_weights[0],
                contract_weights[0],
                cross_weights[0].transpose(1, 0, 2),
            ),
            encoder_half,
        ),
        "section",
    )
    encoder_cotangent, decoder_cotangent = own_rows(output_cotangents)
    decoder_halves = hold(jnp.stack([decoder_half, decoder_cotangent]), encoder_in)
    decoder_others = swap_tensor(decoder_halves) if lax.axis_size("tensor") == 2 else decoder_halves
    ids = lax.dynamic_slice_in_dim(segment_ids, section * rows, rows, 1)
    encoder_ids, decoder_ids = ids[0], ids[1]
    onehots = (bucket_onehot(length, False), bucket_onehot(length, True))
    vectors = [
        jnp.einsum("bh,jb->hj", table, onehot, precision=highest)
        for table, onehot in zip(tables, onehots)
    ]

    x1_part, encoder_self = self_forward(
        encoder_in, gains[0][0], mixing[0], projecting[0], vectors[0], encoder_ids, False
    )
    decoder_halves, decoder_others = hold((decoder_halves, decoder_others), x1_part)
    decoder_in, decoder_cotangent = joined_features(decoder_halves, decoder_others, 2)
    decoder_in = decoder_in.astype(f32)
    z1_part, decoder_self = self_forward(
        decoder_in, gains[1][0], mixing[1], projecting[1], vectors[1], decoder_ids, True
    )
    x1 = encoder_in + total_features(x1_part)
    activated, encoder_dense = dense_forward(hold(x1, z1_part), gains[0][1], expanding[0], contracting[0])
    x2_part = matmul(activated, contracting[0]).astype(bf16)
    z1 = decoder_in + total_features(z1_part)
    cross_in, cross_inverse = norm_forward(z1, gains[1][1])
    query = matmul(cross_in, crossing[1][0]).astype(bf16)[None]
    x2 = x1 + total_features(x2_part)
    encoder_cotangent = gather_features(hold(encoder_cotangent, x2))
    memory_in, memory_inverse = norm_forward(x2, gains[0][2])
    memory = jnp.einsum("td,edc->etc", memory_in, crossing[0], preferred_element_type=f32)
    memory = memory.astype(bf16)
    cross_mixed, cross_logs = attend(
        query, memory, (0, 0, 1), decoder_ids, encoder_ids, None, False
    )
    z2_part = matmul_t(cross_mixed, crossing[1][1]).astype(bf16)
    z2_part, encoder_cotangent = lax.optimization_barrier((z2_part, encoder_cotangent))
    z2 = z1 + total_features(z2_part)
    activated, decoder_dense = dense_forward(z2, gains[1][2], expanding[1], contracting[1])

    before_grad, part = dense_backward(expanding[1], contracting[1], decoder_dense, decoder_cotangent)
    upstream = total_features(part)
    activated, before_grad, normed = hold((activated, before_grad, decoder_dense[0]), part)
    decoder_contract = weight_grad(activated, decoder_cotangent)
    decoder_expand = weight_grad(normed, before_grad)
    upstream = hold(upstream, decoder_contract, decoder_expand)
    first_halves = [section_half(decoder_contract), section_half(decoder_expand)]
    first_sums = sum_rows(first_halves)
    dz2 = norm_backward(z2, gains[1][2], decoder_dense[1], upstream) + decoder_cotangent.astype(f32)
    gain_two = gain_gradient(z2, decoder_dense[1], upstream)

    low = dz2.astype(bf16)
    up = matmul(hold(low, first_halves), crossing[1][1]).astype(bf16)
    dquery, dkeys, dvalues = attend_back(
        query, memory, (0, 0, 1), decoder_ids, encoder_ids, None, False, up, cross_logs
    )
    memory_part = sum(
        matmul_t(part[0], crossing[0][index]) for index, part in enumerate((dkeys, dvalues))
    ).astype(bf16)
    memory_up = total_features(memory_part)
    dquery, dkeys, dvalues, low = hold((dquery, dkeys, dvalues, low), memory_part)
    query_part = matmul_t(dquery[0], crossing[1][0]).astype(bf16)
    decoder_cross = jnp.stack([weight_grad(cross_in, dquery[0]), weight_grad(low, cross_mixed)])
    encoder_cross = jnp.stack(
        [weight_grad(memory_in, dkeys[0]), weight_grad(memory_in, dvalues[0])]
    )

    cross_sum = section_own(encoder_cross, decoder_cross)
    memory_up, decoder_cross, encoder_cross = lax.optimization_barrier(
        (memory_up, decoder_cross, encoder_cross)
    )

    dx2 = norm_backward(x2, gains[0][2], memory_inverse, memory_up) + encoder_cotangent.astype(f32)
    query_own, query_other = exchange(hold(query_part, memory_up))
    low = dx2.astype(bf16)
    before_grad, part = dense_backward(expanding[0], contracting[0], encoder_dense, low)
    upstream = total_features(part)

    before_grad, activated, normed, low, query_own = hold(
        (before_grad, encoder_dense[3], encoder_dense[0], low, query_own), part
    )
    encoder_contract = weight_grad(activated, low)
    encoder_expand = weight_grad(normed, before_grad)
    query_own = hold(query_own, encoder_contract, encoder_expand)
    query_up = total((query_own, query_other))
    dz1 = norm_backward(z1, gains[1][1], cross_inverse, query_up) + dz2
    decoder_low = dz1.astype(bf16)
    decoder_dqkv, decoder_diagonals = self_backward(
        projecting[1], vectors[1], decoder_ids, True, decoder_self, decoder_low
    )

    upstream = hold(upstream, decoder_dqkv)
    dx1 = norm_backward(x1, gains[0][1], encoder_dense[1], upstream) + dx2
    low = dx1.astype(bf16)
    encoder_dqkv, encoder_diagonals = self_backward(
        projecting[0], vectors[0], encoder_ids, False, encoder_self, low
    )

    decoder_dqkv, decoder_low, low = hold((decoder_dqkv, decoder_low, low), encoder_dqkv)
    mixing_sum = [
        weight_own((encoder_self[0], e), (decoder_self[0], d))
        for e, d in zip(encoder_dqkv, decoder_dqkv)
    ]
    projecting_sum = weight_own((encoder_self[3], low), (decoder_self[3], decoder_low))

    encoder_dqkv, decoder_dqkv = hold((encoder_dqkv, decoder_dqkv), mixing_sum, projecting_sum)
    out_part = matmul(decoder_dense[3], contracting[1]).astype(bf16)
    encoder_part = mixing_back(encoder_dqkv, mixing[0])
    decoder_part = mixing_back(decoder_dqkv, mixing[1])

    def narrowed(value, width):
        return jnp.concatenate(
            [value[:, at : at + width] for at in range(0, value.shape[1], width)], axis=0
        )

    def widened(value, width):
        count = width // value.shape[1]
        length = value.shape[0] // count
        return jnp.concatenate(
            [value[at * length : (at + 1) * length] for at in range(count)], axis=1
        )

    contract_sum = section_half(encoder_contract)
    expand_sum = section_half(encoder_expand)
    mixing_sum = jnp.stack(mixing_sum)

    narrow = mixing_sum.shape[2]
    inners = jnp.stack(
        [
            jnp.sum(part.astype(f32) * gain[0] * hidden, axis=1)
            for part, gain, hidden in zip(
                (encoder_part, decoder_part), gains, (encoder_in, decoder_in)
            )
        ]
    )
    kept, received = scatter_begin((encoder_part, decoder_part, out_part))
    inners, other_inners = total_begin(inners)
    groups, kept, inners = lax.optimization_barrier(
        (
            [
                [contract_sum, expand_sum],
                [
                    mixing_sum[:2].reshape(-1, narrow),
                    jnp.concatenate([mixing_sum[2], narrowed(projecting_sum, narrow)]),
                ],
            ],
            kept,
            inners,
        )
    )
    first_sums = hold(first_sums, groups)
    cross_sum = sum_rows(hold(cross_sum, first_sums))
    ring_sum = RingSum(
        [[value.reshape(8, -1, value.shape[1]) for value in pair] for pair in groups]
    )
    ring_sum.step()
    ring_sum.step()
    now = ring_sum.step()

    received, other_inners = hold((received, other_inners), now)
    inners = total_end(inners, other_inners)
    encoder_up, decoder_up, out_sum = scatter_end(kept, received)
    encoder_gain_two = gain_gradient(x2, memory_inverse, memory_up)
    encoder_gain_one = gain_gradient(x1, encoder_dense[1], upstream)
    gain_one = gain_gradient(z1, cross_inverse, query_up)
    encoder_grad, encoder_gain_zero = input_gradient_of(
        encoder_in, gains[0][0], encoder_self[1], encoder_up, inners[0], dx1
    )
    decoder_grad, gain_zero = input_gradient_of(
        decoder_in, gains[1][0], decoder_self[1], decoder_up, inners[1], dz1
    )
    decoder_out = own_features(z2) + out_sum

    def small(gain_zero, gain_one, gain_two, diagonals, onehot):
        ones = [gain_zero[None], own_features(gain_one[None]), own_features(gain_two[None])]
        summed = jnp.sum(diagonals, axis=0).reshape(-1, 2 * length)
        table = jnp.einsum("hj,jb->bh", summed, onehot, precision=highest)
        return jnp.concatenate(ones + [table.reshape(1, -1)], axis=1)

    small_sum = section_own(
        small(
            encoder_gain_zero, encoder_gain_one, encoder_gain_two, encoder_diagonals, onehots[0]
        ),
        small(gain_zero, gain_one, gain_two, decoder_diagonals, onehots[1]),
    )
    mine, give = pick(
        jnp.stack([own_features(x2), encoder_grad]), jnp.stack([decoder_out, decoder_grad])
    )
    other = swap_section(give)
    ring_sum.step()
    ring_sum.step()
    now = ring_sum.step()
    layer_outputs, input_gradient = ordered(section, mine, hold(other, now), 1).reshape(
        2, 1, all_rows, length, local_width
    )
    if ring_sum.around:
        small_sum = small_sum.reshape(-1, 128)
        small_sum = small_sum + hold(swap_y(hold(small_sum, now)), ring_sum.step())
        ring_sum.step()
        small_sum = small_sum + hold(swap_z(small_sum, 1), ring_sum.step())
        ring_sum.step()
        small_sum = small_sum + hold(swap_z(small_sum, 2), ring_sum.step())
        small_sum = small_sum.reshape(-1)
    else:
        small_sum = sum_rows(small_sum).reshape(-1)
    late = ring_sum.step()
    (contract_sum, expand_sum), (query_key_sum, last) = [
        [value.reshape(-1, value.shape[2]) for value in pair] for pair in ring_sum.sums()
    ]
    mixing_sum = jnp.concatenate([query_key_sum, last[:D]]).reshape(3, D, narrow)
    projecting_sum = widened(last[D:], D)
    cross_sum = hold(cross_sum, late)

    def whole(encoder_sum, decoder_sum):
        mine = jnp.where(first, encoder_sum, decoder_sum)
        other = swap_section(jnp.where(first, decoder_sum, encoder_sum))
        return ordered(section, mine, other, 0).astype(f32)

    width = D // lax.axis_size("tensor")
    return (
        layer_outputs,
        input_gradient,
        mixing_sum.astype(f32).transpose(1, 0, 2)[None],
        projecting_sum.astype(f32)[None],
        cross_sum.astype(f32).transpose(1, 0, 2)[None],
        whole(expand_sum, first_sums[1])[None],
        whole(contract_sum, first_sums[0])[None],
        small_sum[: 3 * width].reshape(1, 3, width),
        small_sum[3 * width :].reshape(1, BUCKETS, -1),
    )


def solution(mesh):
    sections, groups, width = mesh.devices.shape
    along = 4 if groups % 4 == 0 else groups
    mesh = Mesh(
        mesh.devices.reshape(sections, along, groups // along, width),
        ("section", "z", "y", "tensor"),
    )
    return jax.shard_map(
        body,
        mesh=mesh,
        in_specs=(
            P("section", ("z", "y"), None, "tensor"),
            P("section", ("z", "y"), None, "tensor"),
            P(None, ("z", "y"), None),
            P("section", None, None, "tensor"),
            P("section", "tensor", None),
            P("section", None, None, "tensor"),
            P("section", None, "tensor"),
            P("section", "tensor", None),
            P("section", None, "tensor"),
            P("section", None, "tensor"),
        ),
        out_specs=(
            P("section", ("z", "y"), None, "tensor"),
            P("section", ("z", "y"), None, "tensor"),
            P("section", None, None, "tensor"),
            P("section", "tensor", None),
            P("section", None, None, "tensor"),
            P("section", None, "tensor"),
            P("section", "tensor", None),
            P("section", None, "tensor"),
            P("section", None, "tensor"),
        ),
        check_vma=False,
    )
```
